512 devices in a mesh: gx: 32 (over z, core), gy: 16 (over y, x).
Axes of the slice: x: 4, y: 4, z: 16, core: 2. Of those that a mesh axis runs over, the one named last changes fastest.
Arguments:
- field: bfloat16 [512, 64, 48, 512], P('gx', None, 'gy'), may hold values from -450 to 450, as said below
- start_one: float32 [512, 128], replicated, may hold values from -6 to 6
- start_two: float32 [512, 128], replicated, may hold values from -6 to 6
Outputs:
- basis_one: float32 [512, 128], replicated
- basis_two: float32 [512, 128], replicated
- core: bfloat16 [128, 64, 48, 128], P(None, 'gx', 'gy')
The draws below stay inside these ranges and needn't reach their ends.
Inputs may be any that keep to these rules, and one draw needn't show every extreme that they name: The field is random, with scales that vary smoothly along each mode, and may contain a few sharp spikes and smooth waves.
All inputs are finite; a program needn't handle non-finite values.
Results may differ from the reference program's by a relative error of at most 0.0075.
Values may be sent and summed in bfloat16 or wider, within the bound.
A program may use at most 64 MiB of HBM per device.

```python
import jax
import jax.numpy as jnp
from jax import lax

N1 = 512
N2 = 512
R = 128
ITERS = 2
N3 = 64
N4 = 48


def mode_factor(key, count, low, high, rise):
    place = jnp.arange(count).astype(jnp.float32) / count
    spread = jnp.exp(jax.random.uniform(key, (count,), jnp.float32, jnp.log(low), jnp.log(high)))
    return spread * jnp.exp(jnp.log(rise) * place)


def draw_field(key, part):
    key = jax.random.fold_in(key, 11)
    keys = jax.random.split(key, 6)
    base = jnp.clip(jax.random.normal(keys[0], (N2, N3, N4, N1), jnp.float32), -4.0, 4.0)
    first = mode_factor(keys[1], N1, 0.5, 3.0, 1.0)
    spot_three = jax.random.randint(keys[5], (3,), 0, N3)
    spot_four = jax.random.randint(jax.random.fold_in(keys[5], 1), (3,), 0, N4)
    third_iota = jnp.arange(N3).astype(jnp.int32)
    fourth_iota = jnp.arange(N4).astype(jnp.int32)
    hits = (third_iota[:, None, None] == spot_three[None, None, :]) & (fourth_iota[None, :, None] == spot_four[None, None, :])
    marked = jnp.any(hits, axis=2).astype(jnp.float32)
    column = jnp.clip(jax.random.normal(jax.random.fold_in(keys[5], 2), (N2,), jnp.float32), -3.0, 3.0)
    row = jnp.clip(jax.random.normal(jax.random.fold_in(keys[5], 3), (N1,), jnp.float32), -3.0, 3.0)
    base = base + 3.0 * column[:, None, None, None] * marked[None, :, :, None] * row[None, None, None, :]
    second = mode_factor(keys[2], N2, 0.5, 2.0, 1.0)
    third = mode_factor(keys[3], N3, 0.7, 1.4, 3.0)
    fourth = mode_factor(keys[4], N4, 0.7, 1.4, 3.0)
    value = base * second[:, None, None, None] * third[None, :, None, None] * fourth[None, None, :, None] * first[None, None, None, :]
    value = jnp.clip(value, -440.0, 440.0)
    return value.astype(jnp.bfloat16)


def bell_draw(own_key, dims, scale, bound, held_as=jnp.bfloat16):
    drawn = jax.random.normal(own_key, dims, jnp.float32) * scale
    return jnp.minimum(jnp.maximum(drawn, -bound), bound).astype(held_as)


def setup_inputs(seed: int = 0) -> dict:
    key_of = jax.random.split(jax.random.key(seed), 4)
    return {
        "field": draw_field(jax.random.fold_in(key_of[3], 71), 0),
        "start_one": bell_draw(key_of[1], (N1, R), 1.0, 6.0, jnp.float32),
        "start_two": bell_draw(key_of[2], (N2, R), 1.0, 6.0, jnp.float32),
    }


def orth(block):
    for turn in range(2):
        inner = jnp.dot(block.T, block, precision=lax.Precision.HIGHEST)
        lower = jnp.linalg.cholesky(inner)
        block = lax.linalg.triangular_solve(lower, block, left_side=False, lower=True, transpose_a=True)
    return block

def leading(gram, start):
    basis = orth(start)
    for step in range(ITERS):
        basis = orth(jnp.dot(gram, basis, precision=lax.Precision.HIGHEST))
    return basis

def reference(field, start_one, start_two):
    size_two, size_three, size_four, size_one = field.shape
    places = jnp.arange(size_three).astype(jnp.int32)

    def gram_step(total, place):
        block = lax.dynamic_index_in_dim(field, place, 1, keepdims=False).reshape(-1, size_one).astype(jnp.float32)
        return (total + jnp.dot(block.T, block, precision=lax.Precision.HIGHEST), None)
    gram_one, unused = lax.scan(gram_step, jnp.zeros((size_one, size_one), jnp.float32), places)
    basis_one = leading(gram_one, start_one)
    narrow_one = basis_one.astype(jnp.bfloat16).astype(jnp.float32)

    def core_step(carry, place):
        block = lax.dynamic_index_in_dim(field, place, 1, keepdims=False).reshape(-1, size_one).astype(jnp.float32)
        part = jnp.dot(block, narrow_one, precision=lax.Precision.HIGHEST).astype(jnp.bfloat16)
        return (carry, part.reshape(size_two, size_four * R))
    unused, core_one = lax.scan(core_step, jnp.float32(0.0), places)

    def second_gram(total, slab):
        block = slab.astype(jnp.float32)
        return (total + jnp.dot(block, block.T, precision=lax.Precision.HIGHEST), None)
    gram_two, unused = lax.scan(second_gram, jnp.zeros((size_two, size_two), jnp.float32), core_one)
    basis_two = leading(gram_two, start_two)
    narrow_two = basis_two.astype(jnp.bfloat16).astype(jnp.float32)

    def final_step(carry, slab):
        part = jnp.dot(narrow_two.T, slab.astype(jnp.float32), precision=lax.Precision.HIGHEST)
        return (carry, part.astype(jnp.bfloat16))
    unused, slabs = lax.scan(final_step, jnp.float32(0.0), core_one)
    core = jnp.transpose(slabs.reshape(size_three, R, size_four, R), (1, 0, 2, 3))
    return (basis_one, basis_two, core)
```

```python
import functools

import jax
import jax.numpy as jnp
from jax import lax
from jax.experimental import pallas as pl
from jax.experimental.pallas import tpu as pltpu
from jax.sharding import PartitionSpec as P

F32 = jnp.float32
BF16 = jnp.bfloat16
HIGHEST = lax.Precision.HIGHEST
MESH = pl.DeviceIdType.MESH
N = 512
R = 128
NX = 32
NY = 16
BLOCKS = [(a, b) for a in range(4) for b in range(a, 4)]
TILES = 160
PER = TILES // NY
GAP = 3
VMEM_LIMIT = 48 * 1024 * 1024


def tree_sum(terms):
    while len(terms) > 1:
        terms = [
            terms[i] + terms[i + 1] if i + 1 < len(terms) else terms[i]
            for i in range(0, len(terms), 2)
        ]
    return terms[0]


def factor_inverse(gram):
    width = 16
    parts = width // 8
    row = lax.broadcasted_iota(jnp.int32, (R, R), 0)
    column = lax.broadcasted_iota(jnp.int32, (R, R), 1)
    diagonal = jnp.where(row == column, gram, 0.0)
    scale_rows = lax.rsqrt(jnp.sum(diagonal, axis=1, keepdims=True))
    scale_columns = lax.rsqrt(jnp.sum(diagonal, axis=0, keepdims=True))
    scaled = gram * scale_rows * scale_columns
    held = [scaled[8 * i : 8 * i + 8, :] for i in range(R // 8)]
    lane = lax.broadcasted_iota(jnp.int32, (8, R), 1)
    sub = lax.broadcasted_iota(jnp.int32, (8, R), 0)

    def along_lanes(x, l):
        return jnp.broadcast_to(x[:, l : l + 1], (8, R))

    def along_subs(x, s):
        return jnp.broadcast_to(x[s : s + 1, :], (8, R))

    out = []
    for k in range(R // width):
        base = k * width
        panel = [held[k * parts + t] for t in range(parts)]
        cols = [[along_lanes(panel[t], base + q) for t in range(parts)] for q in range(width)]
        panel = [
            jnp.where(lane == base + 8 * t + sub, panel[t] + 1.0, panel[t]) for t in range(parts)
        ]
        rows = []
        for j in range(width):
            tj, sj = divmod(j, 8)
            pivot = along_subs(cols[j][tj], sj)
            inverse = 1.0 / pivot
            pivot_row = along_subs(panel[tj], sj)
            kept = jnp.where(lane < base + j, pivot_row, jnp.where(lane == base + j, 1.0, 0.0))
            rows.append(kept * lax.rsqrt(pivot))
            factor = cols[j]
            pivot_row = pivot_row * inverse
            for t in range(parts):
                new = panel[t] - factor[t] * pivot_row
                panel[t] = jnp.where(sub == sj, pivot_row, new) if t == tj else new
            for q in range(j + 1, width):
                entry = along_subs(cols[q][tj], sj) * inverse
                for t in range(parts):
                    new = cols[q][t] - factor[t] * entry
                    cols[q][t] = jnp.where(sub == sj, entry, new) if t == tj else new
        for t in range(parts):
            block = rows[8 * t]
            for s in range(1, 8):
                block = jnp.where(sub >= s, rows[8 * t + s], block)
            out.append(block)
        spread = [along_subs(panel[q // 8], q % 8) for q in range(width)]
        for i in range((k + 1) * parts, R // 8):
            x = held[i]
            held[i] = x - tree_sum([along_lanes(x, base + q) * spread[q] for q in range(width)])
    return jnp.concatenate(out, axis=0) * scale_columns


def dot_tn(a, b, precision=None):
    return lax.dot_general(
        a, b, (((0,), (0,)), ((), ())), precision=precision, preferred_element_type=F32
    )


def dot_nt(a, b, precision=None):
    return lax.dot_general(
        a, b, (((1,), (1,)), ((), ())), precision=precision, preferred_element_type=F32
    )


def orth_pass(y_ref):
    y = y_ref[...]
    y_ref[...] = dot_nt(y, factor_inverse(dot_tn(y, y, HIGHEST)), HIGHEST)


def basis_chain(gram_ref, start_ref, y_ref):
    y_ref[...] = start_ref[...]

    def step(t, carry):
        @pl.when(jnp.logical_and(t >= 2, lax.rem(t, 2) == 0))
        def _():
            y_ref[...] = jnp.dot(
                gram_ref[...], y_ref[...], precision=HIGHEST, preferred_element_type=F32
            )

        orth_pass(y_ref)
        return carry

    lax.fori_loop(0, 6, step, 0)


def enter(gx, gy):
    barrier = pltpu.get_barrier_semaphore()

    def greet_y(d, carry):
        pl.semaphore_signal(
            barrier, inc=1, device_id=(gx, lax.rem(gy + d, NY)), device_id_type=MESH
        )
        return carry

    def greet_x(d, carry):
        pl.semaphore_signal(
            barrier, inc=1, device_id=(lax.rem(gx + d, NX), gy), device_id_type=MESH
        )
        return carry

    lax.fori_loop(1, NY, greet_y, 0)
    lax.fori_loop(1, NX, greet_x, 0)
    return barrier


def remote(src, dst, send, recv, device):
    return pltpu.make_async_remote_copy(
        src_ref=src,
        dst_ref=dst,
        send_sem=send,
        recv_sem=recv,
        device_id=device,
        device_id_type=MESH,
    )


def wait_bytes(ref, sem):
    pltpu.make_async_copy(ref, ref, sem).wait()


def sum_all(gx, gy, tiles, plane_in, line_out, line_in, piece, full, sems):
    s1, r1, s2, r2, s3, r3, s4, r4 = [sems.at[i] for i in range(8)]

    def send_plane(d, carry):
        to = lax.rem(gy + d, NY)
        remote(tiles.at[pl.ds(to * PER, PER)], plane_in.at[gy], s1, r1, (gx, to)).start()
        return carry

    lax.fori_loop(1, NY, send_plane, 0)
    plane_in[gy] = tiles[pl.ds(gy * PER, PER)]
    wait_bytes(plane_in.at[pl.ds(0, NY - 1)], r1)
    line_out[...] = tree_sum([plane_in[p] for p in range(NY)])

    for t in range(PER):
        owner = GAP * t

        @pl.when(gx != owner)
        def _():
            remote(line_out.at[t], line_in.at[gx], s2, r2, (owner, gy)).start()

        @pl.when(gx == owner)
        def _():
            line_in[gx] = line_out[t]

    mine = jnp.logical_and(lax.rem(gx, GAP) == 0, gx < GAP * PER)
    slot = lax.div(gx, GAP)

    @pl.when(mine)
    def _():
        wait_bytes(line_in.at[pl.ds(0, NX - 1)], r2)
        piece[slot] = tree_sum([line_in[p] for p in range(NX)])

        def send_line(d, carry):
            remote(
                piece.at[slot], piece.at[slot], s3, r3, (lax.rem(gx + d, NX), gy)
            ).start()
            return carry

        lax.fori_loop(1, NX, send_line, 0)
        wait_bytes(piece.at[pl.ds(0, PER - 1)], r3)

    @pl.when(jnp.logical_not(mine))
    def _():
        wait_bytes(piece, r3)

    def send_back(d, carry):
        to = lax.rem(gy + d, NY)
        remote(piece, full.at[pl.ds(gy * PER, PER)], s4, r4, (gx, to)).start()
        return carry

    lax.fori_loop(1, NY, send_back, 0)
    full[pl.ds(gy * PER, PER)] = piece[...]
    wait_bytes(full.at[pl.ds(0, TILES - PER)], r4)

    wait_bytes(tiles.at[pl.ds(0, TILES - PER)], s1)
    wait_bytes(full.at[pl.ds(0, TILES - PER)], s4)

    @pl.when(mine)
    def _():
        wait_bytes(line_out.at[pl.ds(0, PER - 1)], s2)
        wait_bytes(line_in.at[pl.ds(0, NX - 1)], s3)

    @pl.when(jnp.logical_not(mine))
    def _():
        wait_bytes(line_out, s2)


SUM_SCRATCH = [
    pltpu.VMEM((TILES, 8, R), F32),
    pltpu.VMEM((NY, PER, 8, R), F32),
    pltpu.VMEM((PER, 8, R), F32),
    pltpu.VMEM((NX, 8, R), F32),
    pltpu.VMEM((PER, 8, R), F32),
    pltpu.VMEM((TILES, 8, R), F32),
    pltpu.SemaphoreType.DMA((8,)),
]


def unpack(full, gram_ref):
    for index, (a, b) in enumerate(BLOCKS):
        block = full[pl.ds(16 * index, 16)].reshape(R, R)
        gram_ref[pl.ds(a * R, R), pl.ds(b * R, R)] = block
        if a != b:
            gram_ref[pl.ds(b * R, R), pl.ds(a * R, R)] = block.T


def gram_one_kernel(x_ref, gram_ref, tiles, plane_in, line_out, line_in, piece, full, sems):
    gx = lax.axis_index("gx")
    gy = lax.axis_index("gy")
    barrier = enter(gx, gy)
    for a in range(4):
        strip = dot_tn(x_ref[:, pl.ds(a * R, R)], x_ref[:, pl.ds(a * R, N - a * R)])
        for b in range(a, 4):
            tiles[pl.ds(16 * BLOCKS.index((a, b)), 16)] = strip[
                :, (b - a) * R : (b - a + 1) * R
            ].reshape(16, 8, R)
    pl.semaphore_wait(barrier, NX + NY - 2)
    sum_all(gx, gy, tiles, plane_in, line_out, line_in, piece, full, sems)
    unpack(full, gram_ref)


def gram_two_kernel(
    x_ref,
    narrow_ref,
    gram_ref,
    flat_ref,
    wide,
    out_slots,
    tiles,
    plane_in,
    line_out,
    line_in,
    piece,
    full,
    sems,
    move_sems,
):
    gx = lax.axis_index("gx")
    gy = lax.axis_index("gy")
    barrier = enter(gx, gy)
    narrow = narrow_ref[...]

    def project(i, carry):
        rows = pl.ds(pl.multiple_of(i * 192, 192), 192)
        wide[rows, :] = jnp.dot(x_ref[rows, :], narrow, preferred_element_type=F32)
        return carry

    lax.fori_loop(0, 16, project, 0)
    pl.semaphore_wait(barrier, NX + NY - 2)

    def regroup(d, carry):
        to = lax.rem(gx + d, NX)
        for k in range(3):
            for j in range(2):
                column = wide[pl.ds(k * 64 + to * 2 + j, 16, stride=192), :]
                out_slots[to, k * 2 + j] = column.astype(BF16)

        @pl.when(d < NX)
        def _():
            remote(
                out_slots.at[to], flat_ref.at[gx], move_sems.at[0], move_sems.at[1], (to, gy)
            ).start()

        return carry

    lax.fori_loop(1, NX + 1, regroup, 0)
    flat_ref[gx] = out_slots[gx]
    wait_bytes(flat_ref.at[pl.ds(0, NX - 1)], move_sems.at[1])
    wait_bytes(out_slots.at[pl.ds(0, NX - 1)], move_sems.at[0])
    for a in range(4):
        strip = None
        for c in range(6):
            left = flat_ref[pl.ds(8 * a, 8), c].reshape(R, R)
            right = flat_ref[pl.ds(8 * a, NX - 8 * a), c].reshape(N - a * R, R)
            part = dot_nt(left, right)
            strip = part if strip is None else strip + part
        for b in range(a, 4):
            tiles[pl.ds(16 * BLOCKS.index((a, b)), 16)] = strip[
                :, (b - a) * R : (b - a + 1) * R
            ].reshape(16, 8, R)
    sum_all(gx, gy, tiles, plane_in, line_out, line_in, piece, full, sems)
    unpack(full, gram_ref)


def chain_one_kernel(gram_ref, start_ref, basis_ref, narrow_ref):
    basis_chain(gram_ref, start_ref, basis_ref)
    narrow_ref[...] = basis_ref[...].astype(BF16)


def chain_two_kernel(gram_ref, start_ref, flat_ref, basis_ref, core_ref):
    basis_chain(gram_ref, start_ref, basis_ref)
    narrow = basis_ref[...].astype(BF16)
    for c in range(6):
        core_ref[c] = dot_tn(narrow, flat_ref[:, c].reshape(N, R)).astype(BF16)


def vmem(count):
    return [pl.BlockSpec(memory_space=pltpu.VMEM)] * count


def call(kernel, outs, inputs, scratch=(), collective=None):
    return pl.pallas_call(
        kernel,
        out_shape=[jax.ShapeDtypeStruct(shape, dtype) for shape, dtype in outs],
        in_specs=vmem(len(inputs)),
        out_specs=vmem(len(outs)),
        scratch_shapes=list(scratch),
        compiler_params=pltpu.CompilerParams(
            collective_id=collective,
            has_side_effects=collective is not None,
            vmem_limit_bytes=VMEM_LIMIT,
        ),
    )(*inputs)


def local(field, start_one, start_two):
    rows = field.transpose(0, 2, 1, 3).reshape(-1, N)
    (gram_one,) = call(gram_one_kernel, [((N, N), F32)], [rows], SUM_SCRATCH, 0)
    basis_one, narrow_one = call(
        chain_one_kernel, [((N, R), F32), ((N, R), BF16)], [gram_one, start_one]
    )
    gram_two, flat_two = call(
        gram_two_kernel,
        [((N, N), F32), ((NX, 6, 16, R), BF16)],
        [rows, narrow_one],
        [pltpu.VMEM((3072, R), F32), pltpu.VMEM((NX, 6, 16, R), BF16)]
        + SUM_SCRATCH
        + [pltpu.SemaphoreType.DMA((2,))],
        1,
    )
    basis_two, core = call(
        chain_two_kernel, [((N, R), F32), ((6, R, R), BF16)], [gram_two, start_two, flat_two]
    )
    core = core.reshape(3, 2, R, R).transpose(2, 1, 0, 3)
    return basis_one, basis_two, core


def solution(mesh):
    placed = (P("gx", None, "gy", None), P(), P())
    return jax.shard_map(
        local,
        mesh=mesh,
        in_specs=placed,
        out_specs=(P(), P(), P(None, "gx", "gy", None)),
        check_vma=False,
    )
```

```python
import functools

import jax
import jax.numpy as jnp
from jax import lax
from jax.experimental import pallas as pl
from jax.experimental.pallas import tpu as pltpu
from jax.sharding import PartitionSpec as P

F32 = jnp.float32
BF16 = jnp.bfloat16
HIGHEST = lax.Precision.HIGHEST
MESH = pl.DeviceIdType.MESH
N = 512
R = 128
NX = 32
NY = 16
BLOCKS = [(a, b) for a in range(4) for b in range(a, 4)]
NZ = NX // 2
GROUP = 2 * NY
TILES = 160
PER = TILES // GROUP
VMEM_LIMIT = 48 * 1024 * 1024


def tree_sum(terms):
    while len(terms) > 1:
        terms = [
            terms[i] + terms[i + 1] if i + 1 < len(terms) else terms[i]
            for i in range(0, len(terms), 2)
        ]
    return terms[0]


def factor_inverse(gram):
    width = 16
    parts = width // 8
    row = lax.broadcasted_iota(jnp.int32, (R, R), 0)
    column = lax.broadcasted_iota(jnp.int32, (R, R), 1)
    diagonal = jnp.where(row == column, gram, 0.0)
    scale_rows = lax.rsqrt(jnp.sum(diagonal, axis=1, keepdims=True))
    scale_columns = lax.rsqrt(jnp.sum(diagonal, axis=0, keepdims=True))
    scaled = gram * scale_rows * scale_columns
    held = [scaled[8 * i : 8 * i + 8, :] for i in range(R // 8)]
    lane = lax.broadcasted_iota(jnp.int32, (8, R), 1)
    sub = lax.broadcasted_iota(jnp.int32, (8, R), 0)

    def along_lanes(x, l):
        return jnp.broadcast_to(x[:, l : l + 1], (8, R))

    def along_subs(x, s):
        return jnp.broadcast_to(x[s : s + 1, :], (8, R))

    out = []
    for k in range(R // width):
        base = k * width
        panel = [held[k * parts + t] for t in range(parts)]
        cols = [[along_lanes(panel[t], base + q) for t in range(parts)] for q in range(width)]
        panel = [
            jnp.where(lane == base + 8 * t + sub, panel[t] + 1.0, panel[t]) for t in range(parts)
        ]
        rows = []
        for j in range(width):
            tj, sj = divmod(j, 8)
            pivot = along_subs(cols[j][tj], sj)
            inverse = 1.0 / pivot
            pivot_row = along_subs(panel[tj], sj)
            kept = jnp.where(lane < base + j, pivot_row, jnp.where(lane == base + j, 1.0, 0.0))
            rows.append(kept * lax.rsqrt(pivot))
            factor = cols[j]
            pivot_row = pivot_row * inverse
            for t in range(parts):
                new = panel[t] - factor[t] * pivot_row
                panel[t] = jnp.where(sub == sj, pivot_row, new) if t == tj else new
            for q in range(j + 1, width):
                entry = along_subs(cols[q][tj], sj) * inverse
                for t in range(parts):
                    new = cols[q][t] - factor[t] * entry
                    cols[q][t] = jnp.where(sub == sj, entry, new) if t == tj else new
        for t in range(parts):
            block = rows[8 * t]
            for s in range(1, 8):
                block = jnp.where(sub >= s, rows[8 * t + s], block)
            out.append(block)
        spread = [along_subs(panel[q // 8], q % 8) for q in range(width)]
        for i in range((k + 1) * parts, R // 8):
            x = held[i]
            held[i] = x - tree_sum([along_lanes(x, base + q) * spread[q] for q in range(width)])
    return jnp.concatenate(out, axis=0) * scale_columns


def dot_tn(a, b, precision=None):
    return lax.dot_general(
        a, b, (((0,), (0,)), ((), ())), precision=precision, preferred_element_type=F32
    )


def dot_nt(a, b, precision=None):
    return lax.dot_general(
        a, b, (((1,), (1,)), ((), ())), precision=precision, preferred_element_type=F32
    )


def orth_pass(y_ref):
    y = y_ref[...]
    y_ref[...] = dot_nt(y, factor_inverse(dot_tn(y, y, HIGHEST)), HIGHEST)


def apply_gram(gram_ref, y_ref):
    y_ref[...] = jnp.dot(gram_ref[...], y_ref[...], precision=HIGHEST, preferred_element_type=F32)


def passes(count, gram_ref, y_ref):
    def step(t, carry):
        if gram_ref is not None:

            @pl.when(lax.rem(t, 2) == 0)
            def _():
                apply_gram(gram_ref, y_ref)

        orth_pass(y_ref)
        return carry

    lax.fori_loop(0, count, step, 0)


def remote(src, dst, send, recv, device):
    return pltpu.make_async_remote_copy(
        src_ref=src,
        dst_ref=dst,
        send_sem=send,
        recv_sem=recv,
        device_id=device,
        device_id_type=MESH,
    )


def wait_bytes(ref, sem):
    pltpu.make_async_copy(ref, ref, sem).wait()


class Place:
    def __init__(self):
        self.gx = lax.axis_index("gx")
        self.gy = lax.axis_index("gy")
        self.z = lax.div(self.gx, 2)
        self.core = lax.rem(self.gx, 2)
        self.member = 2 * self.gy + self.core

    def mate(self, d):
        member = lax.rem(self.member + d, GROUP)
        return member, (2 * self.z + lax.rem(member, 2), lax.div(member, 2))

    def line(self, d):
        return (2 * lax.rem(self.z + d, NZ) + self.core, self.gy)

    def crossed(self, d):
        return (2 * lax.rem(self.z + d, NZ) + 1 - self.core, self.gy)


def enter(place):
    barrier = pltpu.get_barrier_semaphore()

    def greet_mate(d, carry):
        _, device = place.mate(d)
        pl.semaphore_signal(barrier, inc=1, device_id=device, device_id_type=MESH)
        return carry

    def greet_line(d, carry):
        for device in (place.line(d), place.crossed(d)):
            pl.semaphore_signal(barrier, inc=1, device_id=device, device_id_type=MESH)
        return carry

    lax.fori_loop(1, GROUP, greet_mate, 0)
    lax.fori_loop(1, NZ, greet_line, 0)
    pl.semaphore_wait(barrier, GROUP - 1 + 2 * (NZ - 1))


def sum_all(place, bufs, during_plane=None, during_line=None):
    tiles, plane_in, line_out, line_in, piece, full, sent, plane_sems, line_sems, back_sem = bufs

    def send_plane(d, carry):
        member, device = place.mate(d)
        for c in range(PER):
            remote(
                tiles.at[member * PER + c],
                plane_in.at[c, place.member],
                sent.at[0],
                plane_sems.at[c],
                device,
            ).start()
        return carry

    lax.fori_loop(1, GROUP, send_plane, 0)
    if during_plane is not None:
        during_plane()
    for c in range(PER):
        plane_in[c, place.member] = tiles[place.member * PER + c]
        wait_bytes(plane_in.at[c, pl.ds(0, GROUP - 1)], plane_sems.at[c])
        part = tree_sum([plane_in[c, p] for p in range(GROUP)])
        line_out[c] = part
        line_in[c, place.z] = part

        def send_line(d, carry):
            remote(
                line_out.at[c],
                line_in.at[c, place.z],
                sent.at[1],
                line_sems.at[c],
                place.line(lax.rem(d + NZ // 2 - 1, NZ - 1) + 1),
            ).start()
            return carry

        lax.fori_loop(0, NZ - 1, send_line, 0)
    if during_line is not None:
        during_line()
    for c in range(PER):
        wait_bytes(line_in.at[c, pl.ds(0, NZ - 1)], line_sems.at[c])
        total = tree_sum([line_in[c, p] for p in range(NZ)])
        piece[c] = total
        full[place.member * PER + c] = total

        def send_back(d, carry):
            _, device = place.mate(d)
            remote(
                piece.at[c], full.at[place.member * PER + c], sent.at[2], back_sem, device
            ).start()
            return carry

        lax.fori_loop(1, GROUP, send_back, 0)
    wait_bytes(full.at[pl.ds(0, TILES - PER)], back_sem)
    wait_bytes(full.at[pl.ds(0, TILES - PER)], sent.at[0])
    wait_bytes(full.at[pl.ds(0, PER * (NZ - 1))], sent.at[1])
    wait_bytes(full.at[pl.ds(0, TILES - PER)], sent.at[2])


SUM_SCRATCH = [
    pltpu.VMEM((TILES, 8, R), F32),
    pltpu.VMEM((PER, GROUP, 8, R), F32),
    pltpu.VMEM((PER, 8, R), F32),
    pltpu.VMEM((PER, NZ, 8, R), F32),
    pltpu.VMEM((PER, 8, R), F32),
    pltpu.VMEM((TILES, 8, R), F32),
    pltpu.SemaphoreType.DMA((3,)),
    pltpu.SemaphoreType.DMA((PER,)),
    pltpu.SemaphoreType.DMA((PER,)),
    pltpu.SemaphoreType.DMA,
]


def pack(tiles, a, strip):
    for b in range(a, 4):
        tiles[pl.ds(16 * BLOCKS.index((a, b)), 16)] = strip[
            :, (b - a) * R : (b - a + 1) * R
        ].reshape(16, 8, R)


def unpack(full, gram_ref):
    for index, (a, b) in enumerate(BLOCKS):
        block = full[pl.ds(16 * index, 16)].reshape(R, R)
        gram_ref[pl.ds(a * R, R), pl.ds(b * R, R)] = block
        if a != b:
            gram_ref[pl.ds(b * R, R), pl.ds(a * R, R)] = block.T


def main_kernel(x_ref, start_one_ref, start_two_ref, basis_ref, held_two_ref, gram_two_ref, flat_ref, *scratch):
    gram_ref, wide, out_slots, in_slots, move_sems = scratch[:5]
    first = scratch[5 : 5 + len(SUM_SCRATCH)]
    second = scratch[5 + len(SUM_SCRATCH) :]
    place = Place()

    for a in range(4):
        pack(first[0], a, dot_tn(x_ref[:, pl.ds(a * R, R)], x_ref[:, pl.ds(a * R, N - a * R)]))
    enter(place)
    basis_ref[...] = start_one_ref[...]
    sum_all(
        place,
        first,
        during_plane=lambda: orth_pass(basis_ref),
        during_line=lambda: orth_pass(basis_ref),
    )
    unpack(first[5], gram_ref)
    passes(3, gram_ref, basis_ref)

    narrow = basis_ref[...].astype(BF16)

    def project(i, carry):
        rows = pl.ds(pl.multiple_of(i * 192, 192), 192)
        wide[rows, :] = jnp.dot(x_ref[rows, :], narrow, preferred_element_type=F32)
        return carry

    lax.fori_loop(0, 16, project, 0)

    def fill(to):
        for k in range(3):
            for j in range(2):
                column = wide[pl.ds(k * 64 + to * 2 + j, 16, stride=192), :]
                out_slots[to, k * 2 + j] = column.astype(BF16)

    def regroup(d, carry):
        offset = NX // 2 + lax.div(d + 1, 2) * (2 * lax.rem(d, 2) - 1)
        to = lax.rem(place.gx + offset, NX)
        fill(to)
        remote(
            out_slots.at[to],
            in_slots.at[place.gx],
            move_sems.at[0],
            move_sems.at[1],
            (to, place.gy),
        ).start()
        return carry

    lax.fori_loop(0, NX - 1, regroup, 0)
    fill(place.gx)
    in_slots[place.gx] = out_slots[place.gx]

    y = basis_ref[...]
    last = factor_inverse(dot_tn(y, y, HIGHEST))
    basis_ref[...] = dot_nt(y, last, HIGHEST)
    row = lax.broadcasted_iota(jnp.int32, (R, R), 0)
    column = lax.broadcasted_iota(jnp.int32, (R, R), 1)
    change = (last - jnp.where(row == column, 1.0, 0.0)).astype(BF16)
    held_two_ref[...] = start_two_ref[...]
    passes(2, None, held_two_ref)

    wait_bytes(in_slots.at[pl.ds(0, NX - 1)], move_sems.at[1])
    wait_bytes(out_slots.at[pl.ds(0, NX - 1)], move_sems.at[0])
    for c in range(6):
        arrived = in_slots[:, c].reshape(N, R)
        fixed = arrived.astype(F32) + dot_nt(arrived, change)
        flat_ref[:, c] = fixed.astype(BF16).reshape(NX, 16, R)
    for a in range(4):
        strip = None
        for c in range(6):
            left = flat_ref[pl.ds(8 * a, 8), c].reshape(R, R)
            right = flat_ref[pl.ds(8 * a, NX - 8 * a), c].reshape(N - a * R, R)
            part = dot_nt(left, right)
            strip = part if strip is None else strip + part
        pack(second[0], a, strip)
    sum_all(place, second)
    unpack(second[5], gram_two_ref)


def last_kernel(gram_ref, held_ref, flat_ref, basis_ref, core_ref):
    basis_ref[...] = held_ref[...]
    passes(4, gram_ref, basis_ref)
    narrow = basis_ref[...].astype(BF16)
    for c in range(6):
        core_ref[c] = dot_tn(narrow, flat_ref[:, c].reshape(N, R)).astype(BF16)


def vmem(count):
    return [pl.BlockSpec(memory_space=pltpu.VMEM)] * count


def call(kernel, outs, inputs, scratch=(), collective=None):
    return pl.pallas_call(
        kernel,
        out_shape=[jax.ShapeDtypeStruct(shape, dtype) for shape, dtype in outs],
        in_specs=vmem(len(inputs)),
        out_specs=vmem(len(outs)),
        scratch_shapes=list(scratch),
        compiler_params=pltpu.CompilerParams(
            collective_id=collective,
            has_side_effects=collective is not None,
            vmem_limit_bytes=VMEM_LIMIT,
        ),
    )(*inputs)


def local(field, start_one, start_two):
    rows = field.transpose(0, 2, 1, 3).reshape(-1, N)
    basis_one, held_two, gram_two, flat_two = call(
        main_kernel,
        [((N, R), F32), ((N, R), F32), ((N, N), F32), ((NX, 6, 16, R), BF16)],
        [rows, start_one, start_two],
        [
            pltpu.VMEM((N, N), F32),
            pltpu.VMEM((3072, R), F32),
            pltpu.VMEM((NX, 6, 16, R), BF16),
            pltpu.VMEM((NX, 6, 16, R), BF16),
            pltpu.SemaphoreType.DMA((2,)),
        ]
        + SUM_SCRATCH
        + SUM_SCRATCH,
        0,
    )
    basis_two, core = call(
        last_kernel, [((N, R), F32), ((6, R, R), BF16)], [gram_two, held_two, flat_two]
    )
    core = core.reshape(3, 2, R, R).transpose(2, 1, 0, 3)
    return basis_one, basis_two, core


def solution(mesh):
    placed = (P("gx", None, "gy", None), P(), P())
    return jax.shard_map(
        local,
        mesh=mesh,
        in_specs=placed,
        out_specs=(P(), P(), P(None, "gx", "gy", None)),
        check_vma=False,
    )
```

```python
import functools

import jax
import jax.numpy as jnp
from jax import lax
from jax.experimental import pallas as pl
from jax.experimental.pallas import tpu as pltpu
from jax.sharding import PartitionSpec as P

F32 = jnp.float32
BF16 = jnp.bfloat16
HIGHEST = lax.Precision.HIGHEST
MESH = pl.DeviceIdType.MESH
N = 512
R = 128
NX = 32
NY = 16
BLOCKS = [(a, b) for a in range(4) for b in range(a, 4)]
TILES = 160
HALF = TILES // 2
PER = HALF // NY
ROWS = 3072
CHUNK = ROWS // 4
VMEM_LIMIT = 61 * 1024 * 1024


def tree_sum(terms):
    while len(terms) > 1:
        terms = [
            terms[i] + terms[i + 1] if i + 1 < len(terms) else terms[i]
            for i in range(0, len(terms), 2)
        ]
    return terms[0]


def factor_inverse(gram):
    width = 16
    parts = width // 8
    row = lax.broadcasted_iota(jnp.int32, (R, R), 0)
    column = lax.broadcasted_iota(jnp.int32, (R, R), 1)
    diagonal = jnp.where(row == column, gram, 0.0)
    scale_rows = lax.rsqrt(jnp.sum(diagonal, axis=1, keepdims=True))
    scale_columns = lax.rsqrt(jnp.sum(diagonal, axis=0, keepdims=True))
    scaled = gram * scale_rows * scale_columns
    held = [scaled[8 * i : 8 * i + 8, :] for i in range(R // 8)]
    lane = lax.broadcasted_iota(jnp.int32, (8, R), 1)
    sub = lax.broadcasted_iota(jnp.int32, (8, R), 0)

    def along_lanes(x, l):
        return jnp.broadcast_to(x[:, l : l + 1], (8, R))

    def along_subs(x, s):
        return jnp.broadcast_to(x[s : s + 1, :], (8, R))

    out = []
    for k in range(R // width):
        base = k * width
        panel = [held[k * parts + t] for t in range(parts)]
        cols = [[along_lanes(panel[t], base + q) for t in range(parts)] for q in range(width)]
        panel = [
            jnp.where(lane == base + 8 * t + sub, panel[t] + 1.0, panel[t]) for t in range(parts)
        ]
        rows = []
        for j in range(width):
            tj, sj = divmod(j, 8)
            pivot = along_subs(cols[j][tj], sj)
            inverse = 1.0 / pivot
            pivot_row = along_subs(panel[tj], sj)
            kept = jnp.where(lane < base + j, pivot_row, jnp.where(lane == base + j, 1.0, 0.0))
            rows.append(kept * lax.rsqrt(pivot))
            factor = cols[j]
            pivot_row = pivot_row * inverse
            for t in range(parts):
                new = panel[t] - factor[t] * pivot_row
                panel[t] = jnp.where(sub == sj, pivot_row, new) if t == tj else new
            for q in range(j + 1, width):
                entry = along_subs(cols[q][tj], sj) * inverse
                for t in range(parts):
                    new = cols[q][t] - factor[t] * entry
                    cols[q][t] = jnp.where(sub == sj, entry, new) if t == tj else new
        for t in range(parts):
            block = rows[8 * t]
            for s in range(1, 8):
                block = jnp.where(sub >= s, rows[8 * t + s], block)
            out.append(block)
        spread = [along_subs(panel[q // 8], q % 8) for q in range(width)]
        for i in range((k + 1) * parts, R // 8):
            x = held[i]
            held[i] = x - tree_sum([along_lanes(x, base + q) * spread[q] for q in range(width)])
    return jnp.concatenate(out, axis=0) * scale_columns


def dot_tn(a, b, precision=None):
    return lax.dot_general(
        a, b, (((0,), (0,)), ((), ())), precision=precision, preferred_element_type=F32
    )


def dot_nt(a, b, precision=None):
    return lax.dot_general(
        a, b, (((1,), (1,)), ((), ())), precision=precision, preferred_element_type=F32
    )


def orth_pass(y_ref):
    y = y_ref[...]
    y_ref[...] = dot_nt(y, factor_inverse(dot_tn(y, y, HIGHEST)), HIGHEST)


def apply_gram(gram_ref, y_ref):
    y_ref[...] = jnp.dot(gram_ref[...], y_ref[...], precision=HIGHEST, preferred_element_type=F32)


def passes(count, gram_ref, y_ref):
    def step(t, carry):
        if gram_ref is not None:

            @pl.when(lax.rem(t, 2) == 0)
            def _():
                apply_gram(gram_ref, y_ref)

        orth_pass(y_ref)
        return carry

    lax.fori_loop(0, count, step, 0)


def remote(src, dst, send, recv, device):
    return pltpu.make_async_remote_copy(
        src_ref=src,
        dst_ref=dst,
        send_sem=send,
        recv_sem=recv,
        device_id=device,
        device_id_type=MESH,
    )


def wait_bytes(ref, sem):
    pltpu.make_async_copy(ref, ref, sem).wait()


class Place:
    def __init__(self):
        self.gx = lax.axis_index("gx")
        self.gy = lax.axis_index("gy")
        self.z = lax.div(self.gx, 2)
        self.core = lax.rem(self.gx, 2)
        self.quad = lax.rem(self.z, 4)
        self.stride = lax.div(self.z, 4)

    def partner(self):
        return (2 * self.z + 1 - self.core, self.gy)

    def plane(self, d):
        gy = lax.rem(self.gy + d, NY)
        return gy, (self.gx, gy)

    def in_quad(self, d):
        return (2 * (4 * self.stride + lax.rem(self.quad + d, 4)) + self.core, self.gy)

    def in_stride(self, d):
        return (2 * (4 * lax.rem(self.stride + d, 4) + self.quad) + self.core, self.gy)


def greet(place):
    barrier = pltpu.get_barrier_semaphore()

    def greet_line(d, carry):
        device = (lax.rem(place.gx + NX // 2 + d, NX), place.gy)

        @pl.when(d != NX // 2)
        def _():
            pl.semaphore_signal(barrier, inc=1, device_id=device, device_id_type=MESH)

        return carry

    def greet_plane(d, carry):
        _, device = place.plane(d)
        pl.semaphore_signal(barrier, inc=1, device_id=device, device_id_type=MESH)
        return carry

    lax.fori_loop(0, NX, greet_line, 0)
    lax.fori_loop(1, NY, greet_plane, 0)
    return barrier


def sum_all(place, bufs, during_plane=None, during_line=None):
    tiles, core_in, plane_in, quad_out, quad_in, line_out, line_in, piece, full, sent, got = bufs
    own = place.core * HALF
    other = HALF - own

    remote(tiles.at[pl.ds(other, HALF)], core_in, sent.at[0], got.at[0], place.partner()).start()
    wait_bytes(core_in, got.at[0])
    core_in[...] += tiles[pl.ds(own, HALF)]

    def send_plane(d, carry):
        gy, device = place.plane(d)
        remote(
            core_in.at[pl.ds(gy * PER, PER)], plane_in.at[place.gy], sent.at[1], got.at[1], device
        ).start()
        return carry

    lax.fori_loop(1, NY, send_plane, 0)
    plane_in[place.gy] = core_in[pl.ds(place.gy * PER, PER)]
    if during_plane is not None:
        during_plane()
    wait_bytes(plane_in.at[pl.ds(0, NY - 1)], got.at[1])

    part = tree_sum([plane_in[p] for p in range(NY)])
    quad_out[...] = part
    quad_in[place.quad] = part
    for d in (2, 1, 3):
        remote(
            quad_out, quad_in.at[place.quad], sent.at[2], got.at[2], place.in_quad(d)
        ).start()
    wait_bytes(quad_in.at[pl.ds(0, 3)], got.at[2])

    part = tree_sum([quad_in[p] for p in range(4)])
    line_out[...] = part
    line_in[place.stride] = part
    for d in (2, 1, 3):
        remote(
            line_out, line_in.at[place.stride], sent.at[3], got.at[3], place.in_stride(d)
        ).start()
    if during_line is not None:
        during_line()
    wait_bytes(line_in.at[pl.ds(0, 3)], got.at[3])

    total = tree_sum([line_in[p] for p in range(4)])
    piece[...] = total
    here = own + place.gy * PER

    def send_back(d, carry):
        _, device = place.plane(d)
        remote(piece, full.at[pl.ds(here, PER)], sent.at[4], got.at[4], device).start()
        return carry

    lax.fori_loop(1, NY, send_back, 0)
    full[pl.ds(here, PER)] = total
    wait_bytes(full.at[pl.ds(0, HALF - PER)], got.at[4])
    half = full.at[pl.ds(own, HALF)]
    remote(half, half, sent.at[5], got.at[5], place.partner()).start()
    wait_bytes(core_in, got.at[5])

    wait_bytes(core_in, sent.at[0])
    wait_bytes(full.at[pl.ds(0, HALF - PER)], sent.at[1])
    wait_bytes(quad_in.at[pl.ds(0, 3)], sent.at[2])
    wait_bytes(line_in.at[pl.ds(0, 3)], sent.at[3])
    wait_bytes(full.at[pl.ds(0, HALF - PER)], sent.at[4])
    wait_bytes(core_in, sent.at[5])


SUM_SCRATCH = [
    pltpu.VMEM((TILES, 8, R), F32),
    pltpu.VMEM((HALF, 8, R), F32),
    pltpu.VMEM((NY, PER, 8, R), F32),
    pltpu.VMEM((PER, 8, R), F32),
    pltpu.VMEM((4, PER, 8, R), F32),
    pltpu.VMEM((PER, 8, R), F32),
    pltpu.VMEM((4, PER, 8, R), F32),
    pltpu.VMEM((PER, 8, R), F32),
    pltpu.VMEM((TILES, 8, R), F32),
    pltpu.SemaphoreType.DMA((6,)),
    pltpu.SemaphoreType.DMA((6,)),
]


def pack(tiles, a, strip):
    for b in range(a, 4):
        tiles[pl.ds(16 * BLOCKS.index((a, b)), 16)] = strip[
            :, (b - a) * R : (b - a + 1) * R
        ].reshape(16, 8, R)


def unpack(full, gram_ref):
    for index, (a, b) in enumerate(BLOCKS):
        block = full[pl.ds(16 * index, 16)].reshape(R, R)
        gram_ref[pl.ds(a * R, R), pl.ds(b * R, R)] = block
        if a != b:
            gram_ref[pl.ds(b * R, R), pl.ds(a * R, R)] = block.T


def main_kernel(
    field_ref,
    start_one_ref,
    start_two_ref,
    basis_out,
    held_two_out,
    packed_out,
    flat_out,
    *scratch,
):
    (x_ref, gram_ref, wide, out_slots, in_slots, basis_ref, held_two_ref, flat_ref) = scratch[:8]
    load_sems, move_sems, store_sems = scratch[8:11]
    first = scratch[11 : 11 + len(SUM_SCRATCH)]
    second = scratch[11 + len(SUM_SCRATCH) :]
    place = Place()

    loads = [
        pltpu.make_async_copy(
            field_ref.at[pl.ds(q * CHUNK, CHUNK)], x_ref.at[pl.ds(q * CHUNK, CHUNK)], load_sems.at[q]
        )
        for q in range(4)
    ]
    loads.append(pltpu.make_async_copy(start_one_ref, basis_ref, load_sems.at[4]))
    loads.append(pltpu.make_async_copy(start_two_ref, held_two_ref, load_sems.at[5]))
    for load in loads:
        load.start()
    barrier = greet(place)
    strips = [None] * 4
    for q in range(4):
        loads[q].wait()
        rows = pl.ds(q * CHUNK, CHUNK)
        for a in range(4):
            part = dot_tn(x_ref[rows, pl.ds(a * R, R)], x_ref[rows, pl.ds(a * R, N - a * R)])
            strips[a] = part if strips[a] is None else strips[a] + part
    for a in range(4):
        pack(first[0], a, strips[a])
    loads[4].wait()
    loads[5].wait()
    pl.semaphore_wait(barrier, NX + NY - 2)
    sum_all(
        place,
        first,
        during_plane=lambda: orth_pass(basis_ref),
        during_line=lambda: orth_pass(basis_ref),
    )
    unpack(first[8], gram_ref)
    passes(3, gram_ref, basis_ref)

    narrow = basis_ref[...].astype(BF16)

    def project(i, carry):
        rows = pl.ds(pl.multiple_of(i * 192, 192), 192)
        wide[rows, :] = jnp.dot(x_ref[rows, :], narrow, preferred_element_type=F32)
        return carry

    lax.fori_loop(0, 16, project, 0)

    def fill(to):
        for k in range(3):
            for j in range(2):
                column = wide[pl.ds(k * 64 + to * 2 + j, 16, stride=192), :]
                out_slots[to, k * 2 + j] = column.astype(BF16)

    def regroup(d, carry):
        offset = NX // 2 + lax.div(d + 1, 2) * (2 * lax.rem(d, 2) - 1)
        to = lax.rem(place.gx + offset, NX)
        fill(to)
        remote(
            out_slots.at[to],
            in_slots.at[place.gx],
            move_sems.at[0],
            move_sems.at[1],
            (to, place.gy),
        ).start()
        return carry

    lax.fori_loop(0, NX - 1, regroup, 0)
    fill(place.gx)
    in_slots[place.gx] = out_slots[place.gx]

    y = basis_ref[...]
    last = factor_inverse(dot_tn(y, y, HIGHEST))
    basis_ref[...] = dot_nt(y, last, HIGHEST)
    row = lax.broadcasted_iota(jnp.int32, (R, R), 0)
    column = lax.broadcasted_iota(jnp.int32, (R, R), 1)
    change = (last - jnp.where(row == column, 1.0, 0.0)).astype(BF16)
    stores = [pltpu.make_async_copy(basis_ref, basis_out, store_sems.at[0])]
    stores[0].start()
    passes(2, None, held_two_ref)
    stores.append(pltpu.make_async_copy(held_two_ref, held_two_out, store_sems.at[1]))
    stores[1].start()

    wait_bytes(in_slots.at[pl.ds(0, NX - 1)], move_sems.at[1])
    wait_bytes(out_slots.at[pl.ds(0, NX - 1)], move_sems.at[0])
    for c in range(6):
        arrived = in_slots[:, c].reshape(N, R)
        fixed = arrived.astype(F32) + dot_nt(arrived, change)
        flat_ref[:, c] = fixed.astype(BF16).reshape(NX, 16, R)
    stores.append(pltpu.make_async_copy(flat_ref, flat_out, store_sems.at[2]))
    stores[2].start()
    for a in range(4):
        strip = None
        for c in range(6):
            left = flat_ref[pl.ds(8 * a, 8), c].reshape(R, R)
            right = flat_ref[pl.ds(8 * a, NX - 8 * a), c].reshape(N - a * R, R)
            part = dot_nt(left, right)
            strip = part if strip is None else strip + part
        pack(second[0], a, strip)
    sum_all(place, second)
    stores.append(pltpu.make_async_copy(second[8], packed_out, store_sems.at[3]))
    stores[3].start()
    for store in stores:
        store.wait()


def last_kernel(
    packed_in, held_in, flat_in, one_in, basis_ref, core_ref, one_out, packed, gram_ref, flat_ref, sems
):
    copies = [
        pltpu.make_async_copy(source, target, sems.at[i])
        for i, (source, target) in enumerate(
            [(packed_in, packed), (held_in, basis_ref), (flat_in, flat_ref), (one_in, one_out)]
        )
    ]
    for copy in copies:
        copy.start()
    copies[0].wait()
    unpack(packed, gram_ref)
    copies[1].wait()
    passes(4, gram_ref, basis_ref)
    narrow = basis_ref[...].astype(BF16)
    copies[2].wait()
    for c in range(6):
        core_ref[c] = dot_tn(narrow, flat_ref[:, c].reshape(N, R)).astype(BF16)
    copies[3].wait()


def call(kernel, ins, outs, inputs, scratch=(), collective=None):
    return pl.pallas_call(
        kernel,
        out_shape=[jax.ShapeDtypeStruct(shape, dtype) for shape, dtype, _ in outs],
        in_specs=[pl.BlockSpec(memory_space=space) for space in ins],
        out_specs=[pl.BlockSpec(memory_space=space) for _, _, space in outs],
        scratch_shapes=list(scratch),
        compiler_params=pltpu.CompilerParams(
            collective_id=collective,
            has_side_effects=collective is not None,
            vmem_limit_bytes=VMEM_LIMIT,
        ),
    )(*inputs)


def local(field, start_one, start_two):
    rows = field.transpose(0, 2, 1, 3).reshape(-1, N)
    hbm, vmem = pltpu.HBM, pltpu.VMEM
    held_one, held_two, packed_two, flat_two = call(
        main_kernel,
        [hbm] * 3,
        [
            ((N, R), F32, hbm),
            ((N, R), F32, hbm),
            ((TILES, 8, R), F32, hbm),
            ((NX, 6, 16, R), BF16, hbm),
        ],
        [rows, start_one, start_two],
        [
            pltpu.VMEM((ROWS, N), BF16),
            pltpu.VMEM((N, N), F32),
            pltpu.VMEM((ROWS, R), F32),
            pltpu.VMEM((NX, 6, 16, R), BF16),
            pltpu.VMEM((NX, 6, 16, R), BF16),
            pltpu.VMEM((N, R), F32),
            pltpu.VMEM((N, R), F32),
            pltpu.VMEM((NX, 6, 16, R), BF16),
            pltpu.SemaphoreType.DMA((6,)),
            pltpu.SemaphoreType.DMA((2,)),
            pltpu.SemaphoreType.DMA((4,)),
        ]
        + SUM_SCRATCH
        + SUM_SCRATCH,
        0,
    )
    basis_two, core, basis_one = call(
        last_kernel,
        [hbm] * 4,
        [((N, R), F32, vmem), ((6, R, R), BF16, vmem), ((N, R), F32, hbm)],
        [packed_two, held_two, flat_two, held_one],
        [
            pltpu.VMEM((TILES, 8, R), F32),
            pltpu.VMEM((N, N), F32),
            pltpu.VMEM((NX, 6, 16, R), BF16),
            pltpu.SemaphoreType.DMA((4,)),
        ],
    )
    core = core.reshape(3, 2, R, R).transpose(2, 1, 0, 3)
    return basis_one, basis_two, core


def solution(mesh):
    placed = (P("gx", None, "gy", None), P(), P())
    return jax.shard_map(
        local,
        mesh=mesh,
        in_specs=placed,
        out_specs=(P(), P(), P(None, "gx", "gy", None)),
        check_vma=False,
    )
```

```python
import functools

import jax
import jax.numpy as jnp
from jax import lax
from jax.experimental import pallas as pl
from jax.experimental.pallas import tpu as pltpu
from jax.sharding import PartitionSpec as P

F32 = jnp.float32
BF16 = jnp.bfloat16
HIGHEST = lax.Precision.HIGHEST
MESH = pl.DeviceIdType.MESH
N = 512
R = 128
NX = 32
NY = 16
BLOCKS = [(a, b) for a in range(4) for b in range(a, 4)]
TILES = 160
HALF = TILES // 2
PER = HALF // NY
CUTS = ((0, 3), (3, 2))
ROWS = 3072
CHUNK = ROWS // 4


def tree_sum(terms):
    while len(terms) > 1:
        terms = [
            terms[i] + terms[i + 1] if i + 1 < len(terms) else terms[i]
            for i in range(0, len(terms), 2)
        ]
    return terms[0]


def split(x):
    high = x.astype(BF16)
    left = x - high.astype(F32)
    middle = left.astype(BF16)
    return high, middle, (left - middle.astype(F32)).astype(BF16)


def product(x, y):
    pair = jnp.concatenate([y[0], y[1]], axis=1)
    top = dot_nn(x[0], pair)
    second = dot_nn(x[1], pair)
    third = dot_nn(
        jnp.concatenate([x[0], x[2]], axis=1), jnp.concatenate([y[2], y[0]], axis=0)
    )
    return top[:, :R] + (top[:, R:] + second[:, :R] + (second[:, R:] + third))


def gram_of(y):
    high, middle, low = split(y)
    top = dot_tn(high, jnp.concatenate([high, middle], axis=1))
    cross = top[:, R:] + dot_tn(high, low)
    return top[:, :R] + (cross + cross.T + dot_tn(middle, middle))


def factor_inverse(gram):
    width = 16
    parts = width // 8
    row = lax.broadcasted_iota(jnp.int32, (R, R), 0)
    column = lax.broadcasted_iota(jnp.int32, (R, R), 1)
    diagonal = jnp.where(row == column, gram, 0.0)
    scale_rows = lax.rsqrt(jnp.sum(diagonal, axis=1, keepdims=True))
    scale_columns = lax.rsqrt(jnp.sum(diagonal, axis=0, keepdims=True))
    scaled = gram * scale_rows * scale_columns
    held = [scaled[8 * i : 8 * i + 8, :] for i in range(R // 8)]
    lane = lax.broadcasted_iota(jnp.int32, (8, R), 1)
    sub = lax.broadcasted_iota(jnp.int32, (8, R), 0)

    def along_lanes(x, l):
        return jnp.broadcast_to(x[:, l : l + 1], (8, R))

    def along_subs(x, s):
        return jnp.broadcast_to(x[s : s + 1, :], (8, R))

    out = []
    for k in range(R // width):
        base = k * width
        panel = [held[k * parts + t] for t in range(parts)]
        cols = [[along_lanes(panel[t], base + q) for t in range(parts)] for q in range(width)]
        after = range((k + 1) * parts, min((k + 2) * parts, R // 8))
        rest = range((k + 2) * parts, R // 8)
        after_cols = {i: [along_lanes(held[i], base + q) for q in range(width)] for i in after}
        panel = [
            jnp.where(lane == base + 8 * t + sub, panel[t] + 1.0, panel[t]) for t in range(parts)
        ]
        rows = []
        for j in range(width):
            tj, sj = divmod(j, 8)
            pivot = along_subs(cols[j][tj], sj)
            inverse = 1.0 / pivot
            pivot_row = along_subs(panel[tj], sj)
            kept = jnp.where(lane < base + j, pivot_row, jnp.where(lane == base + j, 1.0, 0.0))
            rows.append(kept * lax.rsqrt(pivot))
            factor = cols[j]
            pivot_row = pivot_row * inverse
            for t in range(parts):
                new = panel[t] - factor[t] * pivot_row
                panel[t] = jnp.where(sub == sj, pivot_row, new) if t == tj else new
            for q in range(j + 1, width):
                entry = along_subs(cols[q][tj], sj) * inverse
                for t in range(parts):
                    new = cols[q][t] - factor[t] * entry
                    cols[q][t] = jnp.where(sub == sj, entry, new) if t == tj else new
        for t in range(parts):
            block = rows[8 * t]
            for s in range(1, 8):
                block = jnp.where(sub >= s, rows[8 * t + s], block)
            out.append(block)
        if not after:
            break
        spread = [along_subs(panel[q // 8], q % 8) for q in range(width)]
        for i in after:
            held[i] = held[i] - tree_sum([after_cols[i][q] * spread[q] for q in range(width)])
        if rest:
            x = split(jnp.concatenate([held[i] for i in rest], axis=0))
            y = []
            for part in split(jnp.concatenate(panel, axis=0)):
                above = [jnp.zeros((base, R), BF16)] if base else []
                below = [jnp.zeros((R - base - width, R), BF16)]
                y.append(jnp.concatenate(above + [part] + below, axis=0))
            change = product(x, y)
            for t, i in enumerate(rest):
                held[i] = held[i] - change[8 * t : 8 * t + 8]
    return jnp.concatenate(out, axis=0) * scale_columns


def dot_nn(a, b):
    return jnp.dot(a, b, preferred_element_type=F32)


def dot_tn(a, b, precision=None):
    return lax.dot_general(
        a, b, (((0,), (0,)), ((), ())), precision=precision, preferred_element_type=F32
    )


def dot_nt(a, b, precision=None):
    return lax.dot_general(
        a, b, (((1,), (1,)), ((), ())), precision=precision, preferred_element_type=F32
    )


def orth_pass(y_ref):
    y = y_ref[...]
    y_ref[...] = dot_nt(y, factor_inverse(gram_of(y)), HIGHEST)


def apply_gram(gram_ref, y_ref):
    y_ref[...] = product([gram_ref[i] for i in range(3)], split(y_ref[...]))


def passes(count, gram_ref, y_ref):
    def step(t, carry):
        if gram_ref is not None:

            @pl.when(lax.rem(t, 2) == 0)
            def _():
                apply_gram(gram_ref, y_ref)

        orth_pass(y_ref)
        return carry

    lax.fori_loop(0, count, step, 0)


def remote(src, dst, send, recv, device):
    return pltpu.make_async_remote_copy(
        src_ref=src,
        dst_ref=dst,
        send_sem=send,
        recv_sem=recv,
        device_id=device,
        device_id_type=MESH,
    )


def wait_bytes(ref, sem):
    pltpu.make_async_copy(ref, ref, sem).wait()


class Place:
    def __init__(self):
        self.gx = lax.axis_index("gx")
        self.gy = lax.axis_index("gy")
        self.z = lax.div(self.gx, 2)
        self.core = lax.rem(self.gx, 2)
        self.quad = lax.rem(self.z, 4)
        self.stride = lax.div(self.z, 4)

    def partner(self):
        return (2 * self.z + 1 - self.core, self.gy)

    def plane(self, d):
        gy = lax.rem(self.gy + d, NY)
        return gy, (self.gx, gy)

    def in_quad(self, d):
        return (2 * (4 * self.stride + lax.rem(self.quad + d, 4)) + self.core, self.gy)

    def in_stride(self, d):
        return (2 * (4 * lax.rem(self.stride + d, 4) + self.quad) + self.core, self.gy)


def greet(place):
    barrier = pltpu.get_barrier_semaphore()

    def greet_line(d, carry):
        device = (lax.rem(place.gx + NX // 2 + d, NX), place.gy)

        @pl.when(d != NX // 2)
        def _():
            pl.semaphore_signal(barrier, inc=1, device_id=device, device_id_type=MESH)

        return carry

    def greet_plane(d, carry):
        _, device = place.plane(d)
        pl.semaphore_signal(barrier, inc=1, device_id=device, device_id_type=MESH)
        return carry

    lax.fori_loop(0, NX, greet_line, 0)
    lax.fori_loop(1, NY, greet_plane, 0)
    return barrier


def sum_all(place, bufs, during_plane=None, during_line=None):
    tiles, core_in, plane_in, quad_out, quad_in, line_out, line_in, piece, full, sent, got = bufs
    own = place.core * NY
    other = NY - own

    def part_of(ref, h, *index):
        return ref.at[(*index, pl.ds(*CUTS[h]))]

    for h in range(2):
        remote(
            part_of(tiles, h, pl.ds(other, NY)),
            part_of(core_in, h, pl.ds(0, NY)),
            sent.at[0],
            got.at[0, h],
            place.partner(),
        ).start()
    for h in range(2):
        span = pl.ds(*CUTS[h])
        wait_bytes(part_of(core_in, h, pl.ds(0, NY)), got.at[0, h])
        core_in[:, span] += tiles[pl.ds(own, NY), span]

        def send_plane(d, carry):
            gy, device = place.plane(d)
            remote(
                part_of(core_in, h, gy),
                part_of(plane_in, h, place.gy),
                sent.at[1],
                got.at[1, h],
                device,
            ).start()
            return carry

        lax.fori_loop(1, NY, send_plane, 0)
        plane_in[place.gy, span] = core_in[place.gy, span]
    if during_plane is not None:
        during_plane()
    for h in range(2):
        span = pl.ds(*CUTS[h])
        wait_bytes(part_of(plane_in, h, pl.ds(0, NY - 1)), got.at[1, h])
        part = tree_sum([plane_in[p, span] for p in range(NY)])
        quad_out[span] = part
        quad_in[place.quad, span] = part
        for d in (2, 1, 3):
            remote(
                part_of(quad_out, h),
                part_of(quad_in, h, place.quad),
                sent.at[2],
                got.at[2, h],
                place.in_quad(d),
            ).start()
    for h in range(2):
        span = pl.ds(*CUTS[h])
        wait_bytes(part_of(quad_in, h, pl.ds(0, 3)), got.at[2, h])
        part = tree_sum([quad_in[p, span] for p in range(4)])
        line_out[span] = part
        line_in[place.stride, span] = part
        for d in (2, 1, 3):
            remote(
                part_of(line_out, h),
                part_of(line_in, h, place.stride),
                sent.at[3],
                got.at[3, h],
                place.in_stride(d),
            ).start()
    if during_line is not None:
        during_line()
    here = own + place.gy
    for h in range(2):
        span = pl.ds(*CUTS[h])
        wait_bytes(part_of(line_in, h, pl.ds(0, 3)), got.at[3, h])
        total = tree_sum([line_in[p, span] for p in range(4)])
        piece[span] = total
        full[here, span] = total

        def send_back(d, carry):
            _, device = place.plane(d)
            remote(
                part_of(piece, h), part_of(full, h, here), sent.at[4], got.at[4, h], device
            ).start()
            return carry

        lax.fori_loop(1, NY, send_back, 0)
    for h in range(2):
        wait_bytes(part_of(full, h, pl.ds(0, NY - 1)), got.at[4, h])
        half = part_of(full, h, pl.ds(own, NY))
        remote(half, half, sent.at[5], got.at[5, h], place.partner()).start()
    for h in range(2):
        wait_bytes(part_of(core_in, h, pl.ds(0, NY)), got.at[5, h])

    wait_bytes(core_in, sent.at[0])
    wait_bytes(core_in.at[pl.ds(0, NY - 1)], sent.at[1])
    wait_bytes(quad_in.at[pl.ds(0, 3)], sent.at[2])
    wait_bytes(line_in.at[pl.ds(0, 3)], sent.at[3])
    wait_bytes(core_in.at[pl.ds(0, NY - 1)], sent.at[4])
    wait_bytes(core_in, sent.at[5])


SUM_SCRATCH = [
    pltpu.VMEM((2 * NY, PER, 8, R), F32),
    pltpu.VMEM((NY, PER, 8, R), F32),
    pltpu.VMEM((NY, PER, 8, R), F32),
    pltpu.VMEM((PER, 8, R), F32),
    pltpu.VMEM((4, PER, 8, R), F32),
    pltpu.VMEM((PER, 8, R), F32),
    pltpu.VMEM((4, PER, 8, R), F32),
    pltpu.VMEM((PER, 8, R), F32),
    pltpu.VMEM((2 * NY, PER, 8, R), F32),
    pltpu.SemaphoreType.DMA((6,)),
    pltpu.SemaphoreType.DMA((6, 2)),
]


def pack(tiles, a, strip):
    for b in range(a, 4):
        first = 16 * BLOCKS.index((a, b))
        for t in range(16):
            tiles[(first + t) // PER, (first + t) % PER] = strip[
                8 * t : 8 * t + 8, (b - a) * R : (b - a + 1) * R
            ]


def unpack(full, gram_ref):
    for index, (a, b) in enumerate(BLOCKS):
        block = jnp.concatenate(
            [full[t // PER, t % PER] for t in range(16 * index, 16 * index + 16)], axis=0
        )
        for i, part in enumerate(split(block)):
            gram_ref[i, pl.ds(a * R, R), pl.ds(b * R, R)] = part
        if a != b:
            for i, part in enumerate(split(block.T)):
                gram_ref[i, pl.ds(b * R, R), pl.ds(a * R, R)] = part


def main_kernel(
    field_ref,
    start_one_ref,
    start_two_ref,
    basis_out,
    held_two_out,
    packed_out,
    flat_out,
    *scratch,
):
    (x_ref, gram_ref, wide, out_slots, in_slots, basis_ref, held_two_ref, flat_ref) = scratch[:8]
    load_sems, move_sems, store_sems = scratch[8:11]
    first = scratch[11 : 11 + len(SUM_SCRATCH)]
    second = scratch[11 + len(SUM_SCRATCH) :]
    place = Place()

    loads = [
        pltpu.make_async_copy(
            field_ref.at[pl.ds(q * CHUNK, CHUNK)], x_ref.at[pl.ds(q * CHUNK, CHUNK)], load_sems.at[q]
        )
        for q in range(4)
    ]
    loads.append(pltpu.make_async_copy(start_one_ref, basis_ref, load_sems.at[4]))
    loads.append(pltpu.make_async_copy(start_two_ref, held_two_ref, load_sems.at[5]))
    for load in loads:
        load.start()
    barrier = greet(place)
    strips = [None] * 4
    for q in range(4):
        loads[q].wait()
        rows = pl.ds(q * CHUNK, CHUNK)
        for a in range(4):
            part = dot_tn(x_ref[rows, pl.ds(a * R, R)], x_ref[rows, pl.ds(a * R, N - a * R)])
            strips[a] = part if strips[a] is None else strips[a] + part
    for a in range(4):
        pack(first[0], a, strips[a])
    loads[4].wait()
    loads[5].wait()
    pl.semaphore_wait(barrier, NX + NY - 2)
    sum_all(
        place,
        first,
        during_plane=lambda: orth_pass(basis_ref),
        during_line=lambda: orth_pass(basis_ref),
    )
    unpack(first[8], gram_ref)
    passes(3, gram_ref, basis_ref)

    narrow = basis_ref[...].astype(BF16)

    for q in range(4):
        rows = pl.ds(q * CHUNK, CHUNK)
        wide[rows, :] = dot_nn(x_ref[rows, :], narrow)

    def fill(to):
        for k in range(3):
            for j in range(2):
                column = wide[pl.ds(k * 64 + to * 2 + j, 16, stride=192), :]
                out_slots[to, k * 2 + j] = column.astype(BF16)

    def regroup(d, carry):
        offset = NX // 2 + lax.div(d + 1, 2) * (2 * lax.rem(d, 2) - 1)
        to = lax.rem(place.gx + offset, NX)
        fill(to)
        remote(
            out_slots.at[to],
            in_slots.at[place.gx],
            move_sems.at[0],
            move_sems.at[1],
            (to, place.gy),
        ).start()
        return carry

    lax.fori_loop(0, NX - 1, regroup, 0)
    fill(place.gx)
    in_slots[place.gx] = out_slots[place.gx]

    y = basis_ref[...]
    last = factor_inverse(gram_of(y))
    basis_ref[...] = dot_nt(y, last, HIGHEST)
    row = lax.broadcasted_iota(jnp.int32, (R, R), 0)
    column = lax.broadcasted_iota(jnp.int32, (R, R), 1)
    change = (last - jnp.where(row == column, 1.0, 0.0)).astype(BF16)
    stores = [pltpu.make_async_copy(basis_ref, basis_out, store_sems.at[0])]
    stores[0].start()
    passes(2, None, held_two_ref)
    stores.append(pltpu.make_async_copy(held_two_ref, held_two_out, store_sems.at[1]))
    stores[1].start()

    wait_bytes(in_slots.at[pl.ds(0, NX - 1)], move_sems.at[1])
    wait_bytes(out_slots.at[pl.ds(0, NX - 1)], move_sems.at[0])
    for c in range(6):
        arrived = in_slots[:, c].reshape(N, R)
        fixed = arrived.astype(F32) + dot_nt(arrived, change)
        flat_ref[:, c] = fixed.astype(BF16).reshape(NX, 16, R)
    stores.append(pltpu.make_async_copy(flat_ref, flat_out, store_sems.at[2]))
    stores[2].start()
    for a in range(4):
        strip = None
        for c in range(6):
            left = flat_ref[pl.ds(8 * a, 8), c].reshape(R, R)
            right = flat_ref[pl.ds(8 * a, NX - 8 * a), c].reshape(N - a * R, R)
            part = dot_nt(left, right)
            strip = part if strip is None else strip + part
        pack(second[0], a, strip)
    sum_all(place, second)
    stores.append(pltpu.make_async_copy(second[8], packed_out, store_sems.at[3]))
    stores[3].start()
    for store in stores:
        store.wait()


def last_kernel(
    packed_in, held_in, flat_in, one_in, basis_ref, core_ref, one_out, packed, gram_ref, flat_ref, sems
):
    copies = [
        pltpu.make_async_copy(source, target, sems.at[i])
        for i, (source, target) in enumerate(
            [(packed_in, packed), (held_in, basis_ref), (flat_in, flat_ref), (one_in, one_out)]
        )
    ]
    for copy in copies:
        copy.start()
    copies[0].wait()
    unpack(packed, gram_ref)
    copies[1].wait()
    passes(4, gram_ref, basis_ref)
    narrow = basis_ref[...].astype(BF16)
    copies[2].wait()
    for k in range(3):
        pair = [dot_tn(narrow, flat_ref[:, 2 * k + j].reshape(N, R)) for j in range(2)]
        core_ref[:, k] = jnp.stack(pair, axis=1).astype(BF16)
    copies[3].wait()


def call(kernel, ins, outs, inputs, scratch, collective, limit):
    return pl.pallas_call(
        kernel,
        out_shape=[jax.ShapeDtypeStruct(shape, dtype) for shape, dtype, _ in outs],
        in_specs=[pl.BlockSpec(memory_space=space) for space in ins],
        out_specs=[pl.BlockSpec(memory_space=space) for _, _, space in outs],
        scratch_shapes=list(scratch),
        compiler_params=pltpu.CompilerParams(
            collective_id=collective,
            has_side_effects=collective is not None,
            vmem_limit_bytes=limit * 1024 * 1024,
        ),
    )(*inputs)


def local(field, start_one, start_two):
    rows = field.transpose(0, 2, 1, 3).reshape(-1, N)
    hbm, vmem = pltpu.HBM, pltpu.VMEM
    held_one, held_two, packed_two, flat_two = call(
        main_kernel,
        [hbm] * 3,
        [
            ((N, R), F32, hbm),
            ((N, R), F32, hbm),
            ((2 * NY, PER, 8, R), F32, hbm),
            ((NX, 6, 16, R), BF16, hbm),
        ],
        [rows, start_one, start_two],
        [
            pltpu.VMEM((ROWS, N), BF16),
            pltpu.VMEM((3, N, N), BF16),
            pltpu.VMEM((ROWS, R), F32),
            pltpu.VMEM((NX, 6, 16, R), BF16),
            pltpu.VMEM((NX, 6, 16, R), BF16),
            pltpu.VMEM((N, R), F32),
            pltpu.VMEM((N, R), F32),
            pltpu.VMEM((NX, 6, 16, R), BF16),
            pltpu.SemaphoreType.DMA((6,)),
            pltpu.SemaphoreType.DMA((2,)),
            pltpu.SemaphoreType.DMA((4,)),
        ]
        + SUM_SCRATCH
        + SUM_SCRATCH,
        0,
        61,
    )
    basis_two, core, basis_one = call(
        last_kernel,
        [hbm] * 4,
        [((N, R), F32, vmem), ((R, 3, 2, R), BF16, vmem), ((N, R), F32, hbm)],
        [packed_two, held_two, flat_two, held_one],
        [
            pltpu.VMEM((2 * NY, PER, 8, R), F32),
            pltpu.VMEM((3, N, N), BF16),
            pltpu.VMEM((NX, 6, 16, R), BF16),
            pltpu.SemaphoreType.DMA((4,)),
        ],
        None,
        61,
    )
    return basis_one, basis_two, core.transpose(0, 2, 1, 3)


def solution(mesh):
    placed = (P("gx", None, "gy", None), P(), P())
    return jax.shard_map(
        local,
        mesh=mesh,
        in_specs=placed,
        out_specs=(P(), P(), P(None, "gx", "gy", None)),
        check_vma=False,
    )
```

```python
import functools

import jax
import jax.numpy as jnp
from jax import lax
from jax.experimental import pallas as pl
from jax.experimental.pallas import tpu as pltpu
from jax.sharding import PartitionSpec as P

F32 = jnp.float32
BF16 = jnp.bfloat16
HIGHEST = lax.Precision.HIGHEST
MESH = pl.DeviceIdType.MESH
N = 512
R = 128
NX = 32
NY = 16
BLOCKS = [(a, b) for a in range(4) for b in range(a, 4)]
TILES = 160
HALF = TILES // 2
PER = HALF // NY
CUTS = ((0, 3), (3, 2))
ROWS = 3072
CHUNK = ROWS // 4


def tree_sum(terms):
    while len(terms) > 1:
        terms = [
            terms[i] + terms[i + 1] if i + 1 < len(terms) else terms[i]
            for i in range(0, len(terms), 2)
        ]
    return terms[0]


def split(x):
    high = x.astype(BF16)
    left = x - high.astype(F32)
    middle = left.astype(BF16)
    return high, middle, (left - middle.astype(F32)).astype(BF16)


def product(x, y):
    pair = jnp.concatenate([y[0], y[1]], axis=1)
    top = dot_nn(x[0], pair)
    second = dot_nn(x[1], pair)
    third = dot_nn(
        jnp.concatenate([x[0], x[2]], axis=1), jnp.concatenate([y[2], y[0]], axis=0)
    )
    return top[:, :R] + (top[:, R:] + second[:, :R] + (second[:, R:] + third))


def gram_of(y):
    high, middle, low = split(y)
    top = dot_tn(high, jnp.concatenate([high, middle], axis=1))
    cross = top[:, R:] + dot_tn(high, low)
    return top[:, :R] + (cross + cross.T + dot_tn(middle, middle))


def factor_inverse(gram):
    width = 16
    parts = width // 8
    row = lax.broadcasted_iota(jnp.int32, (R, R), 0)
    column = lax.broadcasted_iota(jnp.int32, (R, R), 1)
    diagonal = jnp.where(row == column, gram, 0.0)
    scale_rows = lax.rsqrt(jnp.sum(diagonal, axis=1, keepdims=True))
    scale_columns = lax.rsqrt(jnp.sum(diagonal, axis=0, keepdims=True))
    scaled = gram * scale_rows * scale_columns
    held = [scaled[8 * i : 8 * i + 8, :] for i in range(R // 8)]
    lane = lax.broadcasted_iota(jnp.int32, (8, R), 1)
    sub = lax.broadcasted_iota(jnp.int32, (8, R), 0)

    def along_lanes(x, l):
        return jnp.broadcast_to(x[:, l : l + 1], (8, R))

    def along_subs(x, s):
        return jnp.broadcast_to(x[s : s + 1, :], (8, R))

    out = []
    for k in range(R // width):
        base = k * width
        panel = [held[k * parts + t] for t in range(parts)]
        cols = [[along_lanes(panel[t], base + q) for t in range(parts)] for q in range(width)]
        after = range((k + 1) * parts, min((k + 2) * parts, R // 8))
        rest = range((k + 2) * parts, R // 8)
        after_cols = {i: [along_lanes(held[i], base + q) for q in range(width)] for i in after}
        panel = [
            jnp.where(lane == base + 8 * t + sub, panel[t] + 1.0, panel[t]) for t in range(parts)
        ]
        rows = []
        for j in range(width):
            tj, sj = divmod(j, 8)
            pivot = along_subs(cols[j][tj], sj)
            inverse = 1.0 / pivot
            pivot_row = along_subs(panel[tj], sj)
            kept = jnp.where(lane < base + j, pivot_row, jnp.where(lane == base + j, 1.0, 0.0))
            rows.append(kept * lax.rsqrt(pivot))
            factor = cols[j]
            pivot_row = pivot_row * inverse
            for t in range(parts):
                new = panel[t] - factor[t] * pivot_row
                panel[t] = jnp.where(sub == sj, pivot_row, new) if t == tj else new
            for q in range(j + 1, width):
                entry = along_subs(cols[q][tj], sj) * inverse
                for t in range(parts):
                    new = cols[q][t] - factor[t] * entry
                    cols[q][t] = jnp.where(sub == sj, entry, new) if t == tj else new
        for t in range(parts):
            block = rows[8 * t]
            for s in range(1, 8):
                block = jnp.where(sub >= s, rows[8 * t + s], block)
            out.append(block)
        if not after:
            break
        spread = [along_subs(panel[q // 8], q % 8) for q in range(width)]
        for i in after:
            held[i] = held[i] - tree_sum([after_cols[i][q] * spread[q] for q in range(width)])
        if rest:
            x = split(jnp.concatenate([held[i] for i in rest], axis=0))
            y = []
            for part in split(jnp.concatenate(panel, axis=0)):
                above = [jnp.zeros((base, R), BF16)] if base else []
                below = [jnp.zeros((R - base - width, R), BF16)]
                y.append(jnp.concatenate(above + [part] + below, axis=0))
            change = product(x, y)
            for t, i in enumerate(rest):
                held[i] = held[i] - change[8 * t : 8 * t + 8]
    return jnp.concatenate(out, axis=0) * scale_columns


def dot_nn(a, b):
    return jnp.dot(a, b, preferred_element_type=F32)


def dot_tn(a, b, precision=None):
    return lax.dot_general(
        a, b, (((0,), (0,)), ((), ())), precision=precision, preferred_element_type=F32
    )


def dot_nt(a, b, precision=None):
    return lax.dot_general(
        a, b, (((1,), (1,)), ((), ())), precision=precision, preferred_element_type=F32
    )


def orth_pass(y_ref):
    y = y_ref[...]
    y_ref[...] = dot_nt(y, factor_inverse(gram_of(y)), HIGHEST)


def apply_gram(gram_ref, y_ref):
    y_ref[...] = product([gram_ref[i] for i in range(3)], split(y_ref[...]))


def passes(count, gram_ref, y_ref):
    def step(t, carry):
        if gram_ref is not None:

            @pl.when(lax.rem(t, 2) == 0)
            def _():
                apply_gram(gram_ref, y_ref)

        orth_pass(y_ref)
        return carry

    lax.fori_loop(0, count, step, 0)


def remote(src, dst, send, recv, device):
    return pltpu.make_async_remote_copy(
        src_ref=src,
        dst_ref=dst,
        send_sem=send,
        recv_sem=recv,
        device_id=device,
        device_id_type=MESH,
    )


def wait_bytes(ref, sem):
    pltpu.make_async_copy(ref, ref, sem).wait()


class Place:
    def __init__(self):
        self.gx = lax.axis_index("gx")
        self.gy = lax.axis_index("gy")
        self.z = lax.div(self.gx, 2)
        self.core = lax.rem(self.gx, 2)
        self.quad = lax.rem(self.z, 4)
        self.stride = lax.div(self.z, 4)

    def far(self, d):
        offset = NX // 2 + lax.div(d + 1, 2) * (2 * lax.rem(d, 2) - 1)
        return lax.rem(self.gx + offset, NX)

    def partner(self):
        return (2 * self.z + 1 - self.core, self.gy)

    def plane(self, d):
        gy = lax.rem(self.gy + d, NY)
        return gy, (self.gx, gy)

    def in_quad(self, d):
        return (2 * (4 * self.stride + lax.rem(self.quad + d, 4)) + self.core, self.gy)

    def in_stride(self, d):
        return (2 * (4 * lax.rem(self.stride + d, 4) + self.quad) + self.core, self.gy)


def greet(place):
    barrier = pltpu.get_barrier_semaphore()

    def greet_line(d, carry):
        device = (lax.rem(place.gx + NX // 2 + d, NX), place.gy)

        @pl.when(d != NX // 2)
        def _():
            pl.semaphore_signal(barrier, inc=1, device_id=device, device_id_type=MESH)

        return carry

    def greet_plane(d, carry):
        _, device = place.plane(d)
        pl.semaphore_signal(barrier, inc=1, device_id=device, device_id_type=MESH)
        return carry

    lax.fori_loop(0, NX, greet_line, 0)
    lax.fori_loop(1, NY, greet_plane, 0)
    return barrier


def sum_all(place, bufs, during_plane=None, during_line=None, during_back=None):
    tiles, core_in, plane_in, quad_out, quad_in, line_out, line_in, piece, full, sent, got = bufs
    own = place.core * NY
    other = NY - own

    def part_of(ref, h, *index):
        return ref.at[(*index, pl.ds(*CUTS[h]))]

    for h in range(2):
        remote(
            part_of(tiles, h, pl.ds(other, NY)),
            part_of(core_in, h, pl.ds(0, NY)),
            sent.at[0],
            got.at[0, h],
            place.partner(),
        ).start()
    for h in range(2):
        span = pl.ds(*CUTS[h])
        wait_bytes(part_of(core_in, h, pl.ds(0, NY)), got.at[0, h])
        core_in[:, span] += tiles[pl.ds(own, NY), span]

        def send_plane(d, carry):
            gy, device = place.plane(d)
            remote(
                part_of(core_in, h, gy),
                part_of(plane_in, h, place.gy),
                sent.at[1],
                got.at[1, h],
                device,
            ).start()
            return carry

        lax.fori_loop(1, NY, send_plane, 0)
        plane_in[place.gy, span] = core_in[place.gy, span]
    if during_plane is not None:
        during_plane()
    for h in range(2):
        span = pl.ds(*CUTS[h])
        wait_bytes(part_of(plane_in, h, pl.ds(0, NY - 1)), got.at[1, h])
        part = tree_sum([plane_in[p, span] for p in range(NY)])
        quad_out[span] = part
        quad_in[place.quad, span] = part
        for d in (2, 1, 3):
            remote(
                part_of(quad_out, h),
                part_of(quad_in, h, place.quad),
                sent.at[2],
                got.at[2, h],
                place.in_quad(d),
            ).start()
    for h in range(2):
        span = pl.ds(*CUTS[h])
        wait_bytes(part_of(quad_in, h, pl.ds(0, 3)), got.at[2, h])
        part = tree_sum([quad_in[p, span] for p in range(4)])
        line_out[span] = part
        line_in[place.stride, span] = part
        for d in (2, 1, 3):
            remote(
                part_of(line_out, h),
                part_of(line_in, h, place.stride),
                sent.at[3],
                got.at[3, h],
                place.in_stride(d),
            ).start()
    if during_line is not None:
        during_line()
    here = own + place.gy
    for h in range(2):
        span = pl.ds(*CUTS[h])
        wait_bytes(part_of(line_in, h, pl.ds(0, 3)), got.at[3, h])
        total = tree_sum([line_in[p, span] for p in range(4)])
        piece[span] = total
        full[here, span] = total

        def send_back(d, carry):
            _, device = place.plane(d)
            remote(
                part_of(piece, h), part_of(full, h, here), sent.at[4], got.at[4, h], device
            ).start()
            return carry

        lax.fori_loop(1, NY, send_back, 0)
    if during_back is not None:
        during_back()
    for h in range(2):
        wait_bytes(part_of(full, h, pl.ds(0, NY - 1)), got.at[4, h])
        half = part_of(full, h, pl.ds(own, NY))
        remote(half, half, sent.at[5], got.at[5, h], place.partner()).start()
    for h in range(2):
        wait_bytes(part_of(core_in, h, pl.ds(0, NY)), got.at[5, h])

    wait_bytes(core_in, sent.at[0])
    wait_bytes(core_in.at[pl.ds(0, NY - 1)], sent.at[1])
    wait_bytes(quad_in.at[pl.ds(0, 3)], sent.at[2])
    wait_bytes(line_in.at[pl.ds(0, 3)], sent.at[3])
    wait_bytes(core_in.at[pl.ds(0, NY - 1)], sent.at[4])
    wait_bytes(core_in, sent.at[5])


SUM_SCRATCH = [
    pltpu.VMEM((2 * NY, PER, 8, R), F32),
    pltpu.VMEM((NY, PER, 8, R), F32),
    pltpu.VMEM((NY, PER, 8, R), F32),
    pltpu.VMEM((PER, 8, R), F32),
    pltpu.VMEM((4, PER, 8, R), F32),
    pltpu.VMEM((PER, 8, R), F32),
    pltpu.VMEM((4, PER, 8, R), F32),
    pltpu.VMEM((PER, 8, R), F32),
    pltpu.VMEM((2 * NY, PER, 8, R), F32),
    pltpu.SemaphoreType.DMA((6,)),
    pltpu.SemaphoreType.DMA((6, 2)),
]


def pack(tiles, a, strip):
    for b in range(a, 4):
        first = 16 * BLOCKS.index((a, b))
        for t in range(16):
            tiles[(first + t) // PER, (first + t) % PER] = strip[
                8 * t : 8 * t + 8, (b - a) * R : (b - a + 1) * R
            ]


def unpack(full, gram_ref):
    for index, (a, b) in enumerate(BLOCKS):
        block = jnp.concatenate(
            [full[t // PER, t % PER] for t in range(16 * index, 16 * index + 16)], axis=0
        )
        for i, part in enumerate(split(block)):
            gram_ref[i, pl.ds(a * R, R), pl.ds(b * R, R)] = part
        if a != b:
            for i, part in enumerate(split(block.T)):
                gram_ref[i, pl.ds(b * R, R), pl.ds(a * R, R)] = part


def main_kernel(
    field_ref,
    start_one_ref,
    start_two_ref,
    basis_out,
    held_two_out,
    packed_out,
    flat_out,
    *scratch,
):
    (x_ref, gram_ref, wide, out_slots, in_slots, basis_ref, held_two_ref, flat_ref) = scratch[:8]
    raw, raw_out, raw_in, load_sems, move_sems, store_sems = scratch[8:14]
    first = scratch[14 : 14 + len(SUM_SCRATCH)]
    second = scratch[14 + len(SUM_SCRATCH) :]
    place = Place()

    loads = [
        pltpu.make_async_copy(
            field_ref.at[pl.ds(q * CHUNK, CHUNK)], x_ref.at[pl.ds(q * CHUNK, CHUNK)], load_sems.at[q]
        )
        for q in range(4)
    ]
    loads.append(pltpu.make_async_copy(start_one_ref, basis_ref, load_sems.at[4]))
    loads.append(pltpu.make_async_copy(start_two_ref, held_two_ref, load_sems.at[5]))
    for load in loads:
        load.start()
    barrier = greet(place)
    strips = [None] * 4
    for q in range(4):
        loads[q].wait()
        rows = pl.ds(q * CHUNK, CHUNK)
        for a in range(4):
            part = dot_tn(x_ref[rows, pl.ds(a * R, R)], x_ref[rows, pl.ds(a * R, N - a * R)])
            strips[a] = part if strips[a] is None else strips[a] + part
    for a in range(4):
        pack(first[0], a, strips[a])
    loads[4].wait()
    loads[5].wait()
    pl.semaphore_wait(barrier, NX + NY - 2)

    def gather_raw():
        def widen(i, carry):
            here = pl.ds(pl.multiple_of(i * 192 + 128, 64), 64)
            there = pl.ds(pl.multiple_of(i * 64, 64), 64)
            for l in range(4):
                raw[l, there] = x_ref[here, pl.ds(l * R, R)].astype(F32)
            return carry

        def pick(to, carry):
            for l in range(4):
                rows = raw[l, pl.ds(2 * to + 1, 16, stride=64), :]
                raw_out[to, :, pl.ds(l * R, R)] = rows.astype(BF16)
            return carry

        lax.fori_loop(0, 16, widen, 0)
        lax.fori_loop(0, NX, pick, 0)
        raw_in[place.gx] = raw_out[place.gx]

    def during_line():
        orth_pass(basis_ref)
        gather_raw()

    def move_raw():
        def send(d, carry):
            to = place.far(d)
            remote(
                raw_out.at[to],
                raw_in.at[place.gx],
                move_sems.at[2],
                move_sems.at[3],
                (to, place.gy),
            ).start()
            return carry

        lax.fori_loop(0, NX - 1, send, 0)

    sum_all(
        place,
        first,
        during_plane=lambda: orth_pass(basis_ref),
        during_line=during_line,
        during_back=move_raw,
    )
    unpack(first[8], gram_ref)
    passes(3, gram_ref, basis_ref)

    narrow = basis_ref[...].astype(BF16)

    for q in range(4):
        rows = pl.ds(q * CHUNK, CHUNK)
        wide[rows, :] = dot_nn(x_ref[rows, :], narrow)

    def fill(to):
        for c in range(5):
            column = wide[pl.ds(c // 2 * 64 + to * 2 + c % 2, 16, stride=192), :]
            out_slots[to, c] = column.astype(BF16)

    def regroup(d, carry):
        to = place.far(d)
        fill(to)
        remote(
            out_slots.at[to],
            in_slots.at[place.gx],
            move_sems.at[0],
            move_sems.at[1],
            (to, place.gy),
        ).start()
        return carry

    lax.fori_loop(0, NX - 1, regroup, 0)
    fill(place.gx)
    in_slots[place.gx] = out_slots[place.gx]

    y = basis_ref[...]
    last = factor_inverse(gram_of(y))
    basis_ref[...] = dot_nt(y, last, HIGHEST)
    row = lax.broadcasted_iota(jnp.int32, (R, R), 0)
    column = lax.broadcasted_iota(jnp.int32, (R, R), 1)
    change = (last - jnp.where(row == column, 1.0, 0.0)).astype(BF16)
    stores = [pltpu.make_async_copy(basis_ref, basis_out, store_sems.at[0])]
    stores[0].start()
    passes(2, None, held_two_ref)
    stores.append(pltpu.make_async_copy(held_two_ref, held_two_out, store_sems.at[1]))
    stores[1].start()

    wait_bytes(raw_in.at[pl.ds(0, NX - 1)], move_sems.at[3])
    wait_bytes(raw_out.at[pl.ds(0, NX - 1)], move_sems.at[2])
    made_here = dot_nn(raw_in[...].reshape(N, N), narrow).astype(BF16)
    wait_bytes(in_slots.at[pl.ds(0, NX - 1)], move_sems.at[1])
    wait_bytes(out_slots.at[pl.ds(0, NX - 1)], move_sems.at[0])
    for c in range(6):
        arrived = in_slots[:, c].reshape(N, R) if c < 5 else made_here
        fixed = arrived.astype(F32) + dot_nt(arrived, change)
        flat_ref[:, c] = fixed.astype(BF16).reshape(NX, 16, R)
    stores.append(pltpu.make_async_copy(flat_ref, flat_out, store_sems.at[2]))
    stores[2].start()
    for a in range(4):
        strip = None
        for c in range(6):
            left = flat_ref[pl.ds(8 * a, 8), c].reshape(R, R)
            right = flat_ref[pl.ds(8 * a, NX - 8 * a), c].reshape(N - a * R, R)
            part = dot_nt(left, right)
            strip = part if strip is None else strip + part
        pack(second[0], a, strip)
    sum_all(place, second)
    stores.append(pltpu.make_async_copy(second[8], packed_out, store_sems.at[3]))
    stores[3].start()
    for store in stores:
        store.wait()


def last_kernel(
    packed_in, held_in, flat_in, one_in, basis_ref, core_ref, one_out, packed, gram_ref, flat_ref, sems
):
    copies = [
        pltpu.make_async_copy(source, target, sems.at[i])
        for i, (source, target) in enumerate(
            [(packed_in, packed), (held_in, basis_ref), (flat_in, flat_ref), (one_in, one_out)]
        )
    ]
    for copy in copies:
        copy.start()
    copies[0].wait()
    unpack(packed, gram_ref)
    copies[1].wait()
    passes(4, gram_ref, basis_ref)
    narrow = basis_ref[...].astype(BF16)
    copies[2].wait()
    for k in range(3):
        pair = [dot_tn(narrow, flat_ref[:, 2 * k + j].reshape(N, R)) for j in range(2)]
        core_ref[:, k] = jnp.stack(pair, axis=1).astype(BF16)
    copies[3].wait()


def call(kernel, ins, outs, inputs, scratch, collective, limit):
    return pl.pallas_call(
        kernel,
        out_shape=[jax.ShapeDtypeStruct(shape, dtype) for shape, dtype, _ in outs],
        in_specs=[pl.BlockSpec(memory_space=space) for space in ins],
        out_specs=[pl.BlockSpec(memory_space=space) for _, _, space in outs],
        scratch_shapes=list(scratch),
        compiler_params=pltpu.CompilerParams(
            collective_id=collective,
            has_side_effects=collective is not None,
            vmem_limit_bytes=limit * 1024 * 1024,
        ),
    )(*inputs)


def local(field, start_one, start_two):
    rows = field.transpose(0, 2, 1, 3).reshape(-1, N)
    hbm, vmem = pltpu.HBM, pltpu.VMEM
    held_one, held_two, packed_two, flat_two = call(
        main_kernel,
        [hbm] * 3,
        [
            ((N, R), F32, hbm),
            ((N, R), F32, hbm),
            ((2 * NY, PER, 8, R), F32, hbm),
            ((NX, 6, 16, R), BF16, hbm),
        ],
        [rows, start_one, start_two],
        [
            pltpu.VMEM((ROWS, N), BF16),
            pltpu.VMEM((3, N, N), BF16),
            pltpu.VMEM((ROWS, R), F32),
            pltpu.VMEM((NX, 5, 16, R), BF16),
            pltpu.VMEM((NX, 5, 16, R), BF16),
            pltpu.VMEM((N, R), F32),
            pltpu.VMEM((N, R), F32),
            pltpu.VMEM((NX, 6, 16, R), BF16),
            pltpu.VMEM((4, 1024, R), F32),
            pltpu.VMEM((NX, 16, N), BF16),
            pltpu.VMEM((NX, 16, N), BF16),
            pltpu.SemaphoreType.DMA((6,)),
            pltpu.SemaphoreType.DMA((4,)),
            pltpu.SemaphoreType.DMA((4,)),
        ]
        + SUM_SCRATCH
        + SUM_SCRATCH,
        0,
        61,
    )
    basis_two, core, basis_one = call(
        last_kernel,
        [hbm] * 4,
        [((N, R), F32, vmem), ((R, 3, 2, R), BF16, vmem), ((N, R), F32, hbm)],
        [packed_two, held_two, flat_two, held_one],
        [
            pltpu.VMEM((2 * NY, PER, 8, R), F32),
            pltpu.VMEM((3, N, N), BF16),
            pltpu.VMEM((NX, 6, 16, R), BF16),
            pltpu.SemaphoreType.DMA((4,)),
        ],
        None,
        61,
    )
    return basis_one, basis_two, core.transpose(0, 2, 1, 3)


def solution(mesh):
    placed = (P("gx", None, "gy", None), P(), P())
    return jax.shard_map(
        local,
        mesh=mesh,
        in_specs=placed,
        out_specs=(P(), P(), P(None, "gx", "gy", None)),
        check_vma=False,
    )
```

```python
import functools

import jax
import jax.numpy as jnp
from jax import lax
from jax.experimental import pallas as pl
from jax.experimental.pallas import tpu as pltpu
from jax.sharding import PartitionSpec as P

F32 = jnp.float32
BF16 = jnp.bfloat16
HIGHEST = lax.Precision.HIGHEST
MESH = pl.DeviceIdType.MESH
N = 512
R = 128
NX = 32
NY = 16
BLOCKS = [(a, b) for a in range(4) for b in range(a, 4)]
TILES = 160
HALF = TILES // 2
PER = HALF // NY
CUTS = ((0, 3), (3, 2))
ROWS = 3072
CHUNK = ROWS // 4


def tree_sum(terms):
    while len(terms) > 1:
        terms = [
            terms[i] + terms[i + 1] if i + 1 < len(terms) else terms[i]
            for i in range(0, len(terms), 2)
        ]
    return terms[0]


def split(x):
    high = x.astype(BF16)
    left = x - high.astype(F32)
    middle = left.astype(BF16)
    return high, middle, (left - middle.astype(F32)).astype(BF16)


def product(x, y):
    pair = jnp.concatenate([y[0], y[1]], axis=1)
    top = dot_nn(x[0], pair)
    second = dot_nn(x[1], pair)
    third = dot_nn(
        jnp.concatenate([x[0], x[2]], axis=1), jnp.concatenate([y[2], y[0]], axis=0)
    )
    return top[:, :R] + (top[:, R:] + second[:, :R] + (second[:, R:] + third))


def gram_of(y):
    high, middle, low = split(y)
    top = dot_tn(high, jnp.concatenate([high, middle], axis=1))
    cross = top[:, R:] + dot_tn(high, low)
    return top[:, :R] + (cross + cross.T + dot_tn(middle, middle))


def factor_inverse(gram):
    width = 16
    parts = width // 8
    row = lax.broadcasted_iota(jnp.int32, (R, R), 0)
    column = lax.broadcasted_iota(jnp.int32, (R, R), 1)
    diagonal = jnp.where(row == column, gram, 0.0)
    scale_rows = lax.rsqrt(jnp.sum(diagonal, axis=1, keepdims=True))
    scale_columns = lax.rsqrt(jnp.sum(diagonal, axis=0, keepdims=True))
    scaled = gram * scale_rows * scale_columns
    held = [scaled[8 * i : 8 * i + 8, :] for i in range(R // 8)]
    lane = lax.broadcasted_iota(jnp.int32, (8, R), 1)
    sub = lax.broadcasted_iota(jnp.int32, (8, R), 0)

    def along_lanes(x, l):
        return jnp.broadcast_to(x[:, l : l + 1], (8, R))

    def along_subs(x, s):
        return jnp.broadcast_to(x[s : s + 1, :], (8, R))

    out = []
    for k in range(R // width):
        base = k * width
        panel = [held[k * parts + t] for t in range(parts)]
        cols = [[along_lanes(panel[t], base + q) for t in range(parts)] for q in range(width)]
        after = range((k + 1) * parts, min((k + 2) * parts, R // 8))
        rest = range((k + 2) * parts, R // 8)
        after_cols = {i: [along_lanes(held[i], base + q) for q in range(width)] for i in after}
        panel = [
            jnp.where(lane == base + 8 * t + sub, panel[t] + 1.0, panel[t]) for t in range(parts)
        ]
        rows = []
        for j in range(width):
            tj, sj = divmod(j, 8)
            pivot = along_subs(cols[j][tj], sj)
            inverse = 1.0 / pivot
            pivot_row = along_subs(panel[tj], sj)
            kept = jnp.where(lane < base + j, pivot_row, jnp.where(lane == base + j, 1.0, 0.0))
            rows.append(kept * lax.rsqrt(pivot))
            factor = cols[j]
            pivot_row = pivot_row * inverse
            for t in range(parts):
                new = panel[t] - factor[t] * pivot_row
                panel[t] = jnp.where(sub == sj, pivot_row, new) if t == tj else new
            for q in range(j + 1, width):
                entry = along_subs(cols[q][tj], sj) * inverse
                for t in range(parts):
                    new = cols[q][t] - factor[t] * entry
                    cols[q][t] = jnp.where(sub == sj, entry, new) if t == tj else new
        for t in range(parts):
            block = rows[8 * t]
            for s in range(1, 8):
                block = jnp.where(sub >= s, rows[8 * t + s], block)
            out.append(block)
        if not after:
            break
        spread = [along_subs(panel[q // 8], q % 8) for q in range(width)]
        for i in after:
            held[i] = held[i] - tree_sum([after_cols[i][q] * spread[q] for q in range(width)])
        if rest:
            x = split(jnp.concatenate([held[i] for i in rest], axis=0))
            y = []
            for part in split(jnp.concatenate(panel, axis=0)):
                above = [jnp.zeros((base, R), BF16)] if base else []
                below = [jnp.zeros((R - base - width, R), BF16)]
                y.append(jnp.concatenate(above + [part] + below, axis=0))
            change = product(x, y)
            for t, i in enumerate(rest):
                held[i] = held[i] - change[8 * t : 8 * t + 8]
    return jnp.concatenate(out, axis=0) * scale_columns


def dot_nn(a, b):
    return jnp.dot(a, b, preferred_element_type=F32)


def dot_tn(a, b, precision=None):
    return lax.dot_general(
        a, b, (((0,), (0,)), ((), ())), precision=precision, preferred_element_type=F32
    )


def dot_nt(a, b, precision=None):
    return lax.dot_general(
        a, b, (((1,), (1,)), ((), ())), precision=precision, preferred_element_type=F32
    )


def orth_pass(y_ref):
    y = y_ref[...]
    y_ref[...] = dot_nt(y, factor_inverse(gram_of(y)), HIGHEST)


def identity():
    row = lax.broadcasted_iota(jnp.int32, (R, R), 0)
    column = lax.broadcasted_iota(jnp.int32, (R, R), 1)
    return jnp.where(row == column, 1.0, 0.0), row, column


def second_pass(y_ref):
    y = y_ref[...]
    gram = gram_of(y)
    one, row, column = identity()
    weight = jnp.where(row > column, 1.0, 0.5 * one)
    error = gram - one
    size = jnp.sum(error * error)
    near = size < 1e-6

    @pl.when(near)
    def _():
        a = error * weight
        narrow = a.astype(BF16)
        second = dot_nn(narrow, narrow) + dot_nt(narrow, narrow) * weight
        y_ref[...] = dot_nt(y, (one - a) + second, HIGHEST)

    @pl.when(jnp.logical_not(near))
    def _():
        y_ref[...] = dot_nt(y, factor_inverse(gram), HIGHEST)


def apply_gram(gram_ref, y_ref):
    y_ref[...] = product([gram_ref[i] for i in range(3)], split(y_ref[...]))


def passes(count, gram_ref, y_ref):
    def step(t, carry):
        if gram_ref is not None:

            @pl.when(lax.rem(t, 2) == 0)
            def _():
                apply_gram(gram_ref, y_ref)

        orth_pass(y_ref)
        return carry

    lax.fori_loop(0, count, step, 0)


def remote(src, dst, send, recv, device):
    return pltpu.make_async_remote_copy(
        src_ref=src,
        dst_ref=dst,
        send_sem=send,
        recv_sem=recv,
        device_id=device,
        device_id_type=MESH,
    )


def wait_bytes(ref, sem):
    pltpu.make_async_copy(ref, ref, sem).wait()


class Place:
    def __init__(self):
        self.gx = lax.axis_index("gx")
        self.gy = lax.axis_index("gy")
        self.z = lax.div(self.gx, 2)
        self.core = lax.rem(self.gx, 2)
        self.quad = lax.rem(self.z, 4)
        self.stride = lax.div(self.z, 4)

    def far(self, d):
        offset = NX // 2 + lax.div(d + 1, 2) * (2 * lax.rem(d, 2) - 1)
        return lax.rem(self.gx + offset, NX)

    def partner(self):
        return (2 * self.z + 1 - self.core, self.gy)

    def plane(self, d):
        gy = lax.rem(self.gy + d, NY)
        return gy, (self.gx, gy)

    def in_quad(self, d):
        return (2 * (4 * self.stride + lax.rem(self.quad + d, 4)) + self.core, self.gy)

    def in_stride(self, d):
        return (2 * (4 * lax.rem(self.stride + d, 4) + self.quad) + self.core, self.gy)


def greet(place):
    barrier = pltpu.get_barrier_semaphore()

    def greet_line(d, carry):
        device = (lax.rem(place.gx + NX // 2 + d, NX), place.gy)

        @pl.when(d != NX // 2)
        def _():
            pl.semaphore_signal(barrier, inc=1, device_id=device, device_id_type=MESH)

        return carry

    def greet_plane(d, carry):
        _, device = place.plane(d)
        pl.semaphore_signal(barrier, inc=1, device_id=device, device_id_type=MESH)
        return carry

    lax.fori_loop(0, NX, greet_line, 0)
    lax.fori_loop(1, NY, greet_plane, 0)
    return barrier


def sum_all(place, bufs, during_plane=None, during_line=None, during_back=None):
    tiles, core_in, plane_in, quad_out, quad_in, line_out, line_in, piece, full, sent, got = bufs
    own = place.core * NY
    other = NY - own

    def part_of(ref, h, *index):
        return ref.at[(*index, pl.ds(*CUTS[h]))]

    for h in range(2):
        remote(
            part_of(tiles, h, pl.ds(other, NY)),
            part_of(core_in, h, pl.ds(0, NY)),
            sent.at[0],
            got.at[0, h],
            place.partner(),
        ).start()
    for h in range(2):
        span = pl.ds(*CUTS[h])
        wait_bytes(part_of(core_in, h, pl.ds(0, NY)), got.at[0, h])
        core_in[:, span] += tiles[pl.ds(own, NY), span]

        def send_plane(d, carry):
            gy, device = place.plane(d)
            remote(
                part_of(core_in, h, gy),
                part_of(plane_in, h, place.gy),
                sent.at[1],
                got.at[1, h],
                device,
            ).start()
            return carry

        lax.fori_loop(1, NY, send_plane, 0)
        plane_in[place.gy, span] = core_in[place.gy, span]
    if during_plane is not None:
        during_plane()
    for h in range(2):
        span = pl.ds(*CUTS[h])
        wait_bytes(part_of(plane_in, h, pl.ds(0, NY - 1)), got.at[1, h])
        part = tree_sum([plane_in[p, span] for p in range(NY)])
        quad_out[span] = part
        quad_in[place.quad, span] = part
        for d in (2, 1, 3):
            remote(
                part_of(quad_out, h),
                part_of(quad_in, h, place.quad),
                sent.at[2],
                got.at[2, h],
                place.in_quad(d),
            ).start()
    for h in range(2):
        span = pl.ds(*CUTS[h])
        wait_bytes(part_of(quad_in, h, pl.ds(0, 3)), got.at[2, h])
        part = tree_sum([quad_in[p, span] for p in range(4)])
        line_out[span] = part
        line_in[place.stride, span] = part
        for d in (2, 1, 3):
            remote(
                part_of(line_out, h),
                part_of(line_in, h, place.stride),
                sent.at[3],
                got.at[3, h],
                place.in_stride(d),
            ).start()
    if during_line is not None:
        during_line()
    here = own + place.gy
    for h in range(2):
        span = pl.ds(*CUTS[h])
        wait_bytes(part_of(line_in, h, pl.ds(0, 3)), got.at[3, h])
        total = tree_sum([line_in[p, span] for p in range(4)])
        piece[span] = total
        full[here, span] = total

        def send_back(d, carry):
            _, device = place.plane(d)
            remote(
                part_of(piece, h), part_of(full, h, here), sent.at[4], got.at[4, h], device
            ).start()
            return carry

        lax.fori_loop(1, NY, send_back, 0)
    if during_back is not None:
        during_back()
    for h in range(2):
        wait_bytes(part_of(full, h, pl.ds(0, NY - 1)), got.at[4, h])
        half = part_of(full, h, pl.ds(own, NY))
        remote(half, half, sent.at[5], got.at[5, h], place.partner()).start()
    for h in range(2):
        wait_bytes(part_of(core_in, h, pl.ds(0, NY)), got.at[5, h])

    wait_bytes(core_in, sent.at[0])
    wait_bytes(core_in.at[pl.ds(0, NY - 1)], sent.at[1])
    wait_bytes(quad_in.at[pl.ds(0, 3)], sent.at[2])
    wait_bytes(line_in.at[pl.ds(0, 3)], sent.at[3])
    wait_bytes(core_in.at[pl.ds(0, NY - 1)], sent.at[4])
    wait_bytes(core_in, sent.at[5])


SUM_SCRATCH = [
    pltpu.VMEM((2 * NY, PER, 8, R), F32),
    pltpu.VMEM((NY, PER, 8, R), F32),
    pltpu.VMEM((NY, PER, 8, R), F32),
    pltpu.VMEM((PER, 8, R), F32),
    pltpu.VMEM((4, PER, 8, R), F32),
    pltpu.VMEM((PER, 8, R), F32),
    pltpu.VMEM((4, PER, 8, R), F32),
    pltpu.VMEM((PER, 8, R), F32),
    pltpu.VMEM((2 * NY, PER, 8, R), F32),
    pltpu.SemaphoreType.DMA((6,)),
    pltpu.SemaphoreType.DMA((6, 2)),
]


def pack(tiles, a, strip):
    for b in range(a, 4):
        first = 16 * BLOCKS.index((a, b))
        for t in range(16):
            tiles[(first + t) // PER, (first + t) % PER] = strip[
                8 * t : 8 * t + 8, (b - a) * R : (b - a + 1) * R
            ]


def unpack(full, gram_ref):
    for index, (a, b) in enumerate(BLOCKS):
        block = jnp.concatenate(
            [full[t // PER, t % PER] for t in range(16 * index, 16 * index + 16)], axis=0
        )
        for i, part in enumerate(split(block)):
            gram_ref[i, pl.ds(a * R, R), pl.ds(b * R, R)] = part
        if a != b:
            for i, part in enumerate(split(block.T)):
                gram_ref[i, pl.ds(b * R, R), pl.ds(a * R, R)] = part


def main_kernel(
    field_ref,
    start_one_ref,
    start_two_ref,
    basis_out,
    held_two_out,
    packed_out,
    flat_out,
    *scratch,
):
    (x_ref, gram_ref, wide, out_slots, in_slots, basis_ref, held_two_ref, flat_ref) = scratch[:8]
    raw, raw_out, raw_in, load_sems, move_sems, store_sems = scratch[8:14]
    first = scratch[14 : 14 + len(SUM_SCRATCH)]
    second = scratch[14 + len(SUM_SCRATCH) :]
    place = Place()

    loads = [
        pltpu.make_async_copy(
            field_ref.at[pl.ds(q * CHUNK, CHUNK)], x_ref.at[pl.ds(q * CHUNK, CHUNK)], load_sems.at[q]
        )
        for q in range(4)
    ]
    loads.append(pltpu.make_async_copy(start_one_ref, basis_ref, load_sems.at[4]))
    loads.append(pltpu.make_async_copy(start_two_ref, held_two_ref, load_sems.at[5]))
    for load in loads:
        load.start()
    barrier = greet(place)
    strips = [None] * 4
    for q in range(4):
        loads[q].wait()
        rows = pl.ds(q * CHUNK, CHUNK)
        for a in range(4):
            part = dot_tn(x_ref[rows, pl.ds(a * R, R)], x_ref[rows, pl.ds(a * R, N - a * R)])
            strips[a] = part if strips[a] is None else strips[a] + part
    for a in range(4):
        pack(first[0], a, strips[a])
    loads[4].wait()
    loads[5].wait()
    pl.semaphore_wait(barrier, NX + NY - 2)

    def gather_raw():
        def widen(i, carry):
            here = pl.ds(pl.multiple_of(i * 192 + 128, 64), 64)
            there = pl.ds(pl.multiple_of(i * 64, 64), 64)
            for l in range(4):
                raw[l, there] = x_ref[here, pl.ds(l * R, R)].astype(F32)
            return carry

        def pick(to, carry):
            for l in range(4):
                rows = raw[l, pl.ds(2 * to + 1, 16, stride=64), :]
                raw_out[to, :, pl.ds(l * R, R)] = rows.astype(BF16)
            return carry

        lax.fori_loop(0, 16, widen, 0)
        lax.fori_loop(0, NX, pick, 0)
        raw_in[place.gx] = raw_out[place.gx]

    def during_line():
        orth_pass(basis_ref)
        gather_raw()

    def move_raw():
        def send(d, carry):
            to = place.far(d)
            remote(
                raw_out.at[to],
                raw_in.at[place.gx],
                move_sems.at[2],
                move_sems.at[3],
                (to, place.gy),
            ).start()
            return carry

        lax.fori_loop(0, NX - 1, send, 0)

    sum_all(
        place,
        first,
        during_plane=lambda: orth_pass(basis_ref),
        during_line=during_line,
        during_back=move_raw,
    )
    unpack(first[8], gram_ref)
    passes(3, gram_ref, basis_ref)

    narrow = basis_ref[...].astype(BF16)

    for q in range(4):
        rows = pl.ds(q * CHUNK, CHUNK)
        wide[rows, :] = dot_nn(x_ref[rows, :], narrow)

    def fill(to):
        for c in range(5):
            column = wide[pl.ds(c // 2 * 64 + to * 2 + c % 2, 16, stride=192), :]
            out_slots[to, c] = column.astype(BF16)

    def regroup(d, carry):
        to = place.far(d)
        fill(to)
        remote(
            out_slots.at[to],
            in_slots.at[place.gx],
            move_sems.at[0],
            move_sems.at[1],
            (to, place.gy),
        ).start()
        return carry

    lax.fori_loop(0, NX - 1, regroup, 0)
    fill(place.gx)
    in_slots[place.gx] = out_slots[place.gx]

    y = basis_ref[...]
    last = factor_inverse(gram_of(y))
    basis_ref[...] = dot_nt(y, last, HIGHEST)
    row = lax.broadcasted_iota(jnp.int32, (R, R), 0)
    column = lax.broadcasted_iota(jnp.int32, (R, R), 1)
    change = (last - jnp.where(row == column, 1.0, 0.0)).astype(BF16)
    stores = [pltpu.make_async_copy(basis_ref, basis_out, store_sems.at[0])]
    stores[0].start()
    passes(2, None, held_two_ref)
    stores.append(pltpu.make_async_copy(held_two_ref, held_two_out, store_sems.at[1]))
    stores[1].start()

    wait_bytes(raw_in.at[pl.ds(0, NX - 1)], move_sems.at[3])
    wait_bytes(raw_out.at[pl.ds(0, NX - 1)], move_sems.at[2])
    made_here = dot_nn(raw_in[...].reshape(N, N), narrow).astype(BF16)
    wait_bytes(in_slots.at[pl.ds(0, NX - 1)], move_sems.at[1])
    wait_bytes(out_slots.at[pl.ds(0, NX - 1)], move_sems.at[0])
    for c in range(6):
        arrived = in_slots[:, c].reshape(N, R) if c < 5 else made_here
        fixed = arrived.astype(F32) + dot_nt(arrived, change)
        flat_ref[:, c] = fixed.astype(BF16).reshape(NX, 16, R)
    stores.append(pltpu.make_async_copy(flat_ref, flat_out, store_sems.at[2]))
    stores[2].start()
    for a in range(4):
        strip = None
        for c in range(6):
            left = flat_ref[pl.ds(8 * a, 8), c].reshape(R, R)
            right = flat_ref[pl.ds(8 * a, NX - 8 * a), c].reshape(N - a * R, R)
            part = dot_nt(left, right)
            strip = part if strip is None else strip + part
        pack(second[0], a, strip)
    sum_all(place, second)
    stores.append(pltpu.make_async_copy(second[8], packed_out, store_sems.at[3]))
    stores[3].start()
    for store in stores:
        store.wait()


def last_kernel(
    packed_in, held_in, flat_in, one_in, basis_ref, core_ref, one_out, packed, gram_ref, flat_ref, sems
):
    copies = [
        pltpu.make_async_copy(source, target, sems.at[i])
        for i, (source, target) in enumerate(
            [(packed_in, packed), (held_in, basis_ref), (flat_in, flat_ref), (one_in, one_out)]
        )
    ]
    for copy in copies:
        copy.start()
    copies[0].wait()
    unpack(packed, gram_ref)
    copies[1].wait()

    def step(t, carry):
        apply_gram(gram_ref, basis_ref)
        orth_pass(basis_ref)
        second_pass(basis_ref)
        return carry

    lax.fori_loop(0, 2, step, 0)
    narrow = basis_ref[...].astype(BF16)
    copies[2].wait()
    for k in range(3):
        pair = [dot_tn(narrow, flat_ref[:, 2 * k + j].reshape(N, R)) for j in range(2)]
        core_ref[:, k] = jnp.stack(pair, axis=1).astype(BF16)
    copies[3].wait()


def call(kernel, ins, outs, inputs, scratch, collective, limit):
    return pl.pallas_call(
        kernel,
        out_shape=[jax.ShapeDtypeStruct(shape, dtype) for shape, dtype, _ in outs],
        in_specs=[pl.BlockSpec(memory_space=space) for space in ins],
        out_specs=[pl.BlockSpec(memory_space=space) for _, _, space in outs],
        scratch_shapes=list(scratch),
        compiler_params=pltpu.CompilerParams(
            collective_id=collective,
            has_side_effects=collective is not None,
            vmem_limit_bytes=limit * 1024 * 1024,
        ),
    )(*inputs)


def local(field, start_one, start_two):
    rows = field.transpose(0, 2, 1, 3).reshape(-1, N)
    hbm, vmem = pltpu.HBM, pltpu.VMEM
    held_one, held_two, packed_two, flat_two = call(
        main_kernel,
        [hbm] * 3,
        [
            ((N, R), F32, hbm),
            ((N, R), F32, hbm),
            ((2 * NY, PER, 8, R), F32, hbm),
            ((NX, 6, 16, R), BF16, hbm),
        ],
        [rows, start_one, start_two],
        [
            pltpu.VMEM((ROWS, N), BF16),
            pltpu.VMEM((3, N, N), BF16),
            pltpu.VMEM((ROWS, R), F32),
            pltpu.VMEM((NX, 5, 16, R), BF16),
            pltpu.VMEM((NX, 5, 16, R), BF16),
            pltpu.VMEM((N, R), F32),
            pltpu.VMEM((N, R), F32),
            pltpu.VMEM((NX, 6, 16, R), BF16),
            pltpu.VMEM((4, 1024, R), F32),
            pltpu.VMEM((NX, 16, N), BF16),
            pltpu.VMEM((NX, 16, N), BF16),
            pltpu.SemaphoreType.DMA((6,)),
            pltpu.SemaphoreType.DMA((4,)),
            pltpu.SemaphoreType.DMA((4,)),
        ]
        + SUM_SCRATCH
        + SUM_SCRATCH,
        0,
        61,
    )
    basis_two, core, basis_one = call(
        last_kernel,
        [hbm] * 4,
        [((N, R), F32, vmem), ((R, 3, 2, R), BF16, vmem), ((N, R), F32, hbm)],
        [packed_two, held_two, flat_two, held_one],
        [
            pltpu.VMEM((2 * NY, PER, 8, R), F32),
            pltpu.VMEM((3, N, N), BF16),
            pltpu.VMEM((NX, 6, 16, R), BF16),
            pltpu.SemaphoreType.DMA((4,)),
        ],
        None,
        61,
    )
    return basis_one, basis_two, core.transpose(0, 2, 1, 3)


def solution(mesh):
    placed = (P("gx", None, "gy", None), P(), P())
    return jax.shard_map(
        local,
        mesh=mesh,
        in_specs=placed,
        out_specs=(P(), P(), P(None, "gx", "gy", None)),
        check_vma=False,
    )
```
